256 devices in a mesh: dp: 64 (over y, z, core), help: 4 (over x).
Axes of the slice: x: 4, y: 4, z: 8, core: 2. Of those that a mesh axis runs over, the one named last changes fastest.
Arguments:
- embeddings: bfloat16 [262144, 768], P(('dp', 'help')), may hold values from -6 to 6
- clusters: int32 [262144], P(('dp', 'help')), may hold values from 0 to 127, as said below
- send_order: int32 [262144], P(('dp', 'help')), may hold values from 0 to 1023, as said below
Outputs:
- nearest: float32 [262144], P(('dp', 'help'))
The draws below stay inside these ranges and needn't reach their ends.
Inputs may be any that keep to these rules, and one draw needn't show every extreme that they name: Cluster c belongs to index c // 2 of dp; every device holds exactly 16 rows of each index's clusters. `send_order`: on each device, a permutation of its local row numbers; positions k * 16 to (k + 1) * 16 - 1 list the rows whose cluster belongs to index k of dp.
All inputs are finite; a program needn't handle non-finite values.
Results may differ from the reference program's by a relative error of at most 0.0014.
Values may be sent and summed in bfloat16 or wider, within the bound.
No kernel may reach another device: no remote copies, remote signals or barrier semaphores. Data moves between devices by JAX's collectives and lax.ppermute only.
A program may use at most 64 MiB of HBM per device.

```python
import jax
import jax.numpy as jnp
from jax import lax

D = 768
ROW_DEV = 1024
CLUST_DEV = 2
SEND = 16
ROWS = 262144
N_DP = 64
N_HELP = 4


def layout(key):
    blocks = N_DP * N_HELP
    send = ROW_DEV // N_DP
    keys = jax.random.split(key, blocks)
    orders = jax.vmap(lambda single: jax.random.permutation(single, ROW_DEV))(keys).astype(jnp.int32)
    label_key = jax.random.fold_in(key, 11)
    within = jax.random.randint(label_key, (blocks, ROW_DEV), 0, CLUST_DEV)
    slots = jnp.arange(ROW_DEV, dtype=jnp.int32)
    block_ids = jnp.arange(blocks, dtype=jnp.int32)[:, None]
    owners = slots // send
    forced = (block_ids // N_HELP + owners[None, :]) % CLUST_DEV
    within = jnp.where((slots % send == 0)[None, :], forced, within)
    labels = (owners[None, :] * CLUST_DEV + within).astype(jnp.int32)
    placed = jax.vmap(lambda order, label: jnp.zeros((ROW_DEV,), jnp.int32).at[order].set(label))(orders, labels)
    return (placed.reshape(-1), orders.reshape(-1))


def draw_clusters(key, part):
    return layout(key)[0]


def draw_send_order(key, part):
    return layout(key)[1]


def shard_levels(stream_key, extent, shards, least, high):
    factor_of, own = 1.0, jax.random.fold_in(stream_key, 6)
    for dim, blocks in shards:
        steps = jnp.exp(jax.random.uniform(jax.random.fold_in(own, dim), (blocks,), jnp.float32, least / len(shards), high / len(shards)))
        factor_of = factor_of * jnp.repeat(steps, extent[dim] // blocks).reshape([-1 if axis == dim else 1 for axis in range(len(extent))])
    return factor_of


def bell_draw(stream_key, extent, width, most, cuts=(), kind=jnp.bfloat16):
    level = shard_levels(stream_key, extent, cuts, -0.22, 0.18) if cuts else 1.0
    drawn = jax.random.normal(stream_key, extent, jnp.float32) * width * level
    return jnp.minimum(jnp.maximum(drawn, -most), most).astype(kind)


def setup_inputs(seed: int = 0) -> dict:
    streams_of = jax.random.split(jax.random.key(seed), 4)
    return {
        "embeddings": bell_draw(streams_of[0], (ROWS, D), 1.0, 6.0, ((0, 256),)),
        "clusters": draw_clusters(jax.random.fold_in(streams_of[3], 71), 0),
        "send_order": draw_send_order(jax.random.fold_in(streams_of[3], 71), 0),
    }


def reference(embeddings, clusters, send_order):
    values = embeddings.astype(jnp.float32)
    unit = (values * lax.rsqrt(lax.optimization_barrier(jnp.sum(values * values, axis=1, keepdims=True)) + 1e-06)).astype(jnp.bfloat16)
    blocks = N_DP * N_HELP
    base = (jnp.arange(blocks, dtype=jnp.int32) * ROW_DEV)[:, None]
    global_rows = (send_order.reshape(blocks, ROW_DEV).astype(jnp.int32) + base).reshape(blocks, N_DP, SEND)
    pools = jnp.transpose(global_rows, (1, 0, 2)).reshape(N_DP, blocks * SEND)

    def owner_pass(index):
        vectors = unit[index]
        labels = clusters[index]
        sims = jnp.dot(vectors, vectors.T, preferred_element_type=jnp.float32)
        mask = (labels[:, None] == labels[None, :]) & (index[None, :] < index[:, None])
        return lax.optimization_barrier(jnp.max(jnp.where(mask, sims, -1.0), axis=1))
    best = lax.map(owner_pass, pools)
    return jnp.zeros((ROWS,), jnp.float32).at[pools.reshape(-1)].set(best.reshape(-1))
```

```python
import jax
import jax.numpy as jnp
from jax import lax
from jax.experimental import pallas as pl
from jax.experimental.pallas import tpu as pltpu
from jax.sharding import PartitionSpec as P

LANES = 128
TILE = 256


def split3(x):
    high = x.astype(jnp.bfloat16)
    rest = x - high.astype(jnp.float32)
    mid = rest.astype(jnp.bfloat16)
    low = (rest - mid.astype(jnp.float32)).astype(jnp.bfloat16)
    return high, mid, low


def iota(shape, dim):
    return lax.broadcasted_iota(jnp.int32, shape, dim)


def dot(a, b, dims):
    return lax.dot_general(a, b, (dims, ((), ())), preferred_element_type=jnp.float32)


def owner_hot(clusters, owners):
    rows = clusters.shape[1]
    return (iota((owners, rows), 0) == clusters // 2).astype(jnp.bfloat16)


def pack_kernel(emb_ref, clu_ref, out_ref, lab_ref, rank_ref):
    rows = emb_ref.shape[0]
    owners = lab_ref.shape[0]
    width = rows // owners
    clusters = clu_ref[...]
    hot = owner_hot(clusters, owners)
    before = (iota((rows, rows), 0) < iota((rows, rows), 1)).astype(jnp.bfloat16)
    count = dot(hot, before, ((1,), (0,)))
    rank = jnp.sum(hot.astype(jnp.float32) * count, axis=0, keepdims=True).astype(jnp.int32)
    rank_ref[...] = rank
    place = (clusters // 2) * width + rank
    bit = (clusters % 2).astype(jnp.float32)
    spots = jnp.where(iota((LANES, rows), 0) == rank, bit, 0.0).astype(jnp.bfloat16)
    lab_ref[...] = dot(hot, spots, ((1,), (1,)))
    values = emb_ref[...].astype(jnp.float32)
    unit = (values * lax.rsqrt(jnp.sum(values * values, axis=1, keepdims=True) + 1e-06)).astype(
        jnp.bfloat16
    )
    for start in range(0, rows, TILE):
        pick = (iota((TILE, rows), 0) + start == place).astype(jnp.bfloat16)
        out_ref[start : start + TILE, :] = dot(pick, unit, ((1,), (0,))).astype(jnp.bfloat16)


def pack(embeddings, clusters, owners):
    rows, depth = embeddings.shape
    return pl.pallas_call(
        pack_kernel,
        out_shape=(
            jax.ShapeDtypeStruct((rows, depth), jnp.bfloat16),
            jax.ShapeDtypeStruct((owners, LANES), jnp.float32),
            jax.ShapeDtypeStruct((1, rows), jnp.int32),
        ),
        compiler_params=pltpu.CompilerParams(vmem_limit_bytes=48 * 2**20),
        name="pack",
    )(embeddings, clusters.reshape(1, rows))


def row_labels(lab, rows, width):
    owners = lab.shape[0]
    hot = (iota((owners, rows), 0) == iota((owners, rows), 1) // width).astype(jnp.bfloat16)
    spread = dot(lab.astype(jnp.bfloat16), hot, ((0,), (0,)))
    chosen = iota((LANES, rows), 0) == iota((LANES, rows), 1) % width
    return jnp.sum(jnp.where(chosen, spread, 0.0), axis=0, keepdims=True)


def column_labels(lab, rows, width):
    owners = lab.shape[0]
    hot = (iota((rows, owners), 1) == iota((rows, owners), 0) // width).astype(jnp.bfloat16)
    spread = dot(hot, lab.astype(jnp.bfloat16), ((1,), (0,)))
    chosen = iota((rows, LANES), 1) == iota((rows, LANES), 0) % width
    kept = jnp.where(chosen, spread, 0.0).astype(jnp.bfloat16)
    return dot(kept, jnp.ones((LANES, TILE), jnp.bfloat16), ((1,), (0,)))


def pair_best(query_ref, key_ref, query_labels, key_labels_ref, limit):
    rows = query_ref.shape[0]
    parts = []
    for start in range(0, rows, TILE):
        queries = query_ref[start : start + TILE, :]
        labels = query_labels[:, start : start + TILE]
        best = jnp.full((1, TILE), -1.0, jnp.float32)
        for low in range(0, start + TILE, TILE):
            sims = dot(key_ref[low : low + TILE, :], queries, ((1,), (1,)))
            mask = key_labels_ref[low : low + TILE, :] == labels
            if low == start:
                mask = mask & (iota((TILE, TILE), 0) + low < limit[:, start : start + TILE])
            sims = jnp.where(mask, sims, -1.0)
            best = jnp.maximum(best, jnp.max(sims, axis=0, keepdims=True))
        parts.append(best)
    return jnp.concatenate(parts, axis=1)


def limit_of(rows, width, query_help, key_help):
    place = iota((1, rows), 1)
    group = place // width * width
    return jnp.where(
        key_help == query_help, place, jnp.where(key_help < query_help, group + width, group)
    )


def store_groups(out_ref, best, width):
    owners = out_ref.shape[0]
    rows = best.shape[1]
    mine = iota((owners, rows), 0) == iota((owners, rows), 1) // width
    spots = (iota((rows, LANES), 0) % width == iota((rows, LANES), 1)).astype(jnp.bfloat16)
    total = jnp.zeros((owners, LANES), jnp.float32)
    for piece in split3(best):
        spread = jnp.where(mine, piece.astype(jnp.float32), 0.0).astype(jnp.bfloat16)
        total = total + dot(spread, spots, ((1,), (0,)))
    out_ref[...] = total


def cross_kernel(help_ref, left_ref, right_ref, lab_left_ref, lab_right_ref, out_ref, col_ref):
    rows = left_ref.shape[0]
    width = rows // lab_left_ref.shape[0]
    me, helpers = help_ref[0], help_ref[1]
    left, right = lax.rem(me + helpers - 1, helpers), lax.rem(me + 1, helpers)
    col_ref[...] = column_labels(lab_right_ref[...], rows, width)
    best = pair_best(
        left_ref,
        right_ref,
        row_labels(lab_left_ref[...], rows, width),
        col_ref,
        limit_of(rows, width, left, right),
    )
    store_groups(out_ref, best, width)


def own_kernel(
    help_ref, own_ref, left_ref, right_ref, lab_ref, lab_left_ref, lab_right_ref, out_ref, col_ref
):
    rows = own_ref.shape[0]
    width = rows // lab_ref.shape[0]
    me, helpers = help_ref[0], help_ref[1]
    left, right = lax.rem(me + helpers - 1, helpers), lax.rem(me + 1, helpers)
    labels = row_labels(lab_ref[...], rows, width)
    best = None
    for key_ref, key_lab_ref, place in (
        (own_ref, lab_ref, me),
        (left_ref, lab_left_ref, left),
        (right_ref, lab_right_ref, right),
    ):
        col_ref[...] = column_labels(key_lab_ref[...], rows, width)
        found = pair_best(own_ref, key_ref, labels, col_ref, limit_of(rows, width, me, place))
        best = found if best is None else jnp.maximum(best, found)
    store_groups(out_ref, best, width)


def sims_call(kernel, name, where, arrays, labels):
    rows = arrays[0].shape[0]
    vmem = pl.BlockSpec(memory_space=pltpu.VMEM)
    return pl.pallas_call(
        kernel,
        out_shape=jax.ShapeDtypeStruct(labels[0].shape, jnp.float32),
        in_specs=[pl.BlockSpec(memory_space=pltpu.SMEM)] + [vmem] * (len(arrays) + len(labels)),
        out_specs=vmem,
        scratch_shapes=[pltpu.VMEM((rows, TILE), jnp.float32)],
        compiler_params=pltpu.CompilerParams(vmem_limit_bytes=48 * 2**20),
        name=name,
    )(where, *arrays, *labels)


def unpack_kernel(clu_ref, rank_ref, res_ref, out_ref):
    owners = res_ref.shape[0]
    rows = clu_ref.shape[1]
    hot = owner_hot(clu_ref[...], owners)
    total = jnp.zeros((LANES, rows), jnp.float32)
    for piece in split3(res_ref[...]):
        total = total + dot(piece, hot, ((0,), (0,)))
    mine = iota((LANES, rows), 0) == rank_ref[...]
    out_ref[...] = jnp.sum(jnp.where(mine, total, 0.0), axis=0, keepdims=True)


def unpack(clusters, rank, result):
    rows = clusters.shape[0]
    return pl.pallas_call(
        unpack_kernel,
        out_shape=jax.ShapeDtypeStruct((1, rows), jnp.float32),
        name="unpack",
    )(clusters.reshape(1, rows), rank, result).reshape(rows)


def shards(embeddings, clusters, send_order):
    rows, depth = embeddings.shape
    owners = lax.axis_size("dp")
    helpers = lax.axis_size("help")
    width = rows // owners
    up = [(h, (h + 1) % helpers) for h in range(helpers)]
    down = [(h, (h - 1) % helpers) for h in range(helpers)]
    where = jnp.stack([lax.axis_index("help"), jnp.int32(helpers)])
    outgoing, out_labels, rank = pack(embeddings, clusters, owners)
    own = lax.all_to_all(
        outgoing.reshape(owners, width, depth), "dp", split_axis=0, concat_axis=0, tiled=True
    ).reshape(rows, depth)
    lab = lax.all_to_all(
        out_labels.reshape(owners, 1, LANES), "dp", split_axis=0, concat_axis=0, tiled=True
    ).reshape(owners, LANES)
    lab_left, lab_right = lax.ppermute(lab, "help", up), lax.ppermute(lab, "help", down)
    left, right = lax.ppermute(own, "help", up), lax.ppermute(own, "help", down)
    cross = sims_call(cross_kernel, "cross", where, (left, right), (lab_left, lab_right))
    cross = lax.ppermute(cross, "help", down)
    best = sims_call(own_kernel, "own", where, (own, left, right), (lab, lab_left, lab_right))
    best = jnp.maximum(best, cross)
    returned = lax.all_to_all(
        best.reshape(owners, 1, LANES), "dp", split_axis=0, concat_axis=0, tiled=True
    ).reshape(owners, LANES)
    return unpack(clusters, rank, returned)


def solution(mesh):
    return jax.shard_map(
        shards,
        mesh=mesh,
        in_specs=(P(("dp", "help"), None), P(("dp", "help")), P(("dp", "help"))),
        out_specs=P(("dp", "help")),
        check_vma=False,
    )
```

```python
import jax
import jax.numpy as jnp
from jax import lax
from jax.experimental import pallas as pl
from jax.experimental.pallas import tpu as pltpu
from jax.sharding import PartitionSpec as P

LANES = 128
TILE = 256


def split3(x):
    high = x.astype(jnp.bfloat16)
    rest = x - high.astype(jnp.float32)
    mid = rest.astype(jnp.bfloat16)
    low = (rest - mid.astype(jnp.float32)).astype(jnp.bfloat16)
    return high, mid, low


def iota(shape, dim):
    return lax.broadcasted_iota(jnp.int32, shape, dim)


def dot(a, b, dims):
    return lax.dot_general(a, b, (dims, ((), ())), preferred_element_type=jnp.float32)


def slot_of(clusters, core, half):
    owner = clusters // 2
    away = jnp.where(owner // half == core, 0, 1)
    return owner % half + away * half, away


def pack_kernel(where_ref, emb_ref, clu_ref, keep_ref, send_ref, keep_lab_ref, send_lab_ref, spot_ref):
    rows = emb_ref.shape[0]
    half = keep_lab_ref.shape[0]
    width = keep_ref.shape[0] // half
    clusters = clu_ref[...]
    slot, away = slot_of(clusters, where_ref[1], half)
    hot = (iota((2 * half, rows), 0) == slot).astype(jnp.bfloat16)
    before = (iota((rows, rows), 0) < iota((rows, rows), 1)).astype(jnp.bfloat16)
    count = dot(hot, before, ((1,), (0,)))
    rank = jnp.sum(hot.astype(jnp.float32) * count, axis=0, keepdims=True).astype(jnp.int32)
    spot = rank + away * width
    spot_ref[...] = spot
    place = slot * width + rank
    bit = (clusters % 2).astype(jnp.float32)
    spots = jnp.where(iota((LANES, rows), 0) == spot, bit, 0.0).astype(jnp.bfloat16)
    labels = dot(hot, spots, ((1,), (1,)))
    keep_lab_ref[...] = labels[:half]
    send_lab_ref[...] = labels[half:]
    values = emb_ref[...].astype(jnp.float32)
    unit = (values * lax.rsqrt(jnp.sum(values * values, axis=1, keepdims=True) + 1e-06)).astype(
        jnp.bfloat16
    )
    for out_ref, base in ((send_ref, rows // 2), (keep_ref, 0)):
        for start in range(0, rows // 2, TILE):
            pick = (iota((TILE, rows), 0) + (base + start) == place).astype(jnp.bfloat16)
            out_ref[start : start + TILE, :] = dot(pick, unit, ((1,), (0,))).astype(jnp.bfloat16)


def pack(where, embeddings, clusters, owners):
    rows, depth = embeddings.shape
    vmem = pl.BlockSpec(memory_space=pltpu.VMEM)
    return pl.pallas_call(
        pack_kernel,
        out_shape=(
            jax.ShapeDtypeStruct((rows // 2, depth), jnp.bfloat16),
            jax.ShapeDtypeStruct((rows // 2, depth), jnp.bfloat16),
            jax.ShapeDtypeStruct((owners // 2, LANES), jnp.float32),
            jax.ShapeDtypeStruct((owners // 2, LANES), jnp.float32),
            jax.ShapeDtypeStruct((1, rows), jnp.int32),
        ),
        in_specs=[pl.BlockSpec(memory_space=pltpu.SMEM), vmem, vmem],
        compiler_params=pltpu.CompilerParams(vmem_limit_bytes=48 * 2**20),
        name="pack",
    )(where, embeddings, clusters.reshape(1, rows))


def order_of(place, core, part):
    source, flip, rank = place // 32, place // 16 % 2, place % 16
    from_core = jnp.where(flip == 0, core, 1 - core)
    by_row = (source * 2 + from_core) * 4 + part
    by_column = ((part * 8 + source // 4) * 2 + from_core) * 4 + source % 4
    return jnp.where(core == 0, by_row, by_column) * 16 + rank


def row_labels(lab, rows):
    sources = lab.shape[0]
    width = rows // sources
    hot = (iota((sources, rows), 0) == iota((sources, rows), 1) // width).astype(jnp.bfloat16)
    spread = dot(lab.astype(jnp.bfloat16), hot, ((0,), (0,)))
    chosen = iota((LANES, rows), 0) == iota((LANES, rows), 1) % width
    return jnp.sum(jnp.where(chosen, spread, 0.0), axis=0, keepdims=True)


def column_labels(lab, rows):
    sources = lab.shape[0]
    width = rows // sources
    hot = (iota((rows, sources), 1) == iota((rows, sources), 0) // width).astype(jnp.bfloat16)
    spread = dot(hot, lab.astype(jnp.bfloat16), ((1,), (0,)))
    chosen = iota((rows, LANES), 1) == iota((rows, LANES), 0) % width
    kept = jnp.where(chosen, spread, 0.0).astype(jnp.bfloat16)
    return dot(kept, jnp.ones((LANES, LANES), jnp.bfloat16), ((1,), (0,)))


def set_keys(order_ref, labels_ref, lab_ref, core, part):
    rows = order_ref.shape[0]
    order_ref[...] = order_of(iota((rows, LANES), 0), core, part)
    labels_ref[...] = column_labels(lab_ref[...], rows)


def scan(best_ref, query_ref, key_ref, query_labels, order_ref, labels_ref, core, part, pick):
    rows = query_ref.shape[0]
    order = order_of(iota((1, rows), 1), core, part)
    for start in range(0, rows, TILE):
        queries = query_ref[start : start + TILE, :]
        here = slice(start, start + TILE)
        best = best_ref[:, here]
        for low in range(0, rows, TILE):
            if not pick(low, start):
                continue
            sims = dot(key_ref[low : low + TILE, :], queries, ((1,), (1,)))
            wide = (
                jnp.concatenate([ref[low : low + TILE, :]] * (TILE // LANES), axis=1)
                for ref in (order_ref, labels_ref)
            )
            key_order, key_labels = wide
            mask = (key_labels == query_labels[:, here]) & (key_order < order[:, here])
            found = jnp.max(jnp.where(mask, sims, -1.0), axis=0, keepdims=True)
            best = jnp.maximum(best, found)
        best_ref[:, here] = best


def scan_pair(best_ref, query_ref, key_ref, query_labels, order_ref, labels_ref, core, part, key_part):
    args = (best_ref, query_ref, key_ref, query_labels, order_ref, labels_ref, core, part)

    @pl.when((core == 0) | (key_part < part))
    def _():
        scan(*args, lambda low, start: low <= start)

    @pl.when((core != 0) & (key_part < part))
    def _():
        scan(*args, lambda low, start: low > start)


def store_groups(out_ref, best):
    sources = out_ref.shape[0]
    rows = best.shape[1]
    width = rows // sources
    mine = iota((sources, rows), 0) == iota((sources, rows), 1) // width
    spots = (iota((rows, LANES), 0) % width == iota((rows, LANES), 1)).astype(jnp.bfloat16)
    total = jnp.zeros((sources, LANES), jnp.float32)
    for piece in split3(best):
        spread = jnp.where(mine, piece.astype(jnp.float32), 0.0).astype(jnp.bfloat16)
        total = total + dot(spread, spots, ((1,), (0,)))
    out_ref[...] = total


def parts_of(where_ref):
    me, core, parts = where_ref[0], where_ref[1], where_ref[2]
    return core, me, lax.rem(me + parts - 1, parts), lax.rem(me + 1, parts)


def alone_kernel(where_ref, own_ref, lab_ref, best_ref, order_ref, labels_ref):
    rows = own_ref.shape[0]
    core, me, _, _ = parts_of(where_ref)
    best_ref[...] = jnp.full((1, rows), -1.0, jnp.float32)
    set_keys(order_ref, labels_ref, lab_ref, core, me)
    scan(
        best_ref, own_ref, own_ref, row_labels(lab_ref[...], rows), order_ref, labels_ref, core, me,
        lambda low, start: low <= start,
    )


def cross_kernel(where_ref, left_ref, right_ref, lab_left_ref, lab_right_ref, out_ref, best_ref, order_ref, labels_ref):
    rows = left_ref.shape[0]
    core, _, left, right = parts_of(where_ref)
    best_ref[...] = jnp.full((1, rows), -1.0, jnp.float32)
    set_keys(order_ref, labels_ref, lab_left_ref, core, left)
    labels = row_labels(lab_right_ref[...], rows)
    scan_pair(best_ref, right_ref, left_ref, labels, order_ref, labels_ref, core, right, left)
    store_groups(out_ref, best_ref[...])


def sides_kernel(
    where_ref, alone_ref, own_ref, left_ref, right_ref, lab_ref, lab_left_ref, lab_right_ref,
    out_ref, best_ref, order_ref, labels_ref,
):
    rows = own_ref.shape[0]
    core, me, left, right = parts_of(where_ref)
    best_ref[...] = alone_ref[...]
    labels = row_labels(lab_ref[...], rows)
    for key_ref, key_lab_ref, part in ((left_ref, lab_left_ref, left), (right_ref, lab_right_ref, right)):
        set_keys(order_ref, labels_ref, key_lab_ref, core, part)
        scan_pair(best_ref, own_ref, key_ref, labels, order_ref, labels_ref, core, me, part)
    store_groups(out_ref, best_ref[...])


def sims_call(kernel, name, out_shape, where, arrays, rows, scratch):
    vmem = pl.BlockSpec(memory_space=pltpu.VMEM)
    best = [pltpu.VMEM((1, rows), jnp.float32)] if scratch else []
    return pl.pallas_call(
        kernel,
        out_shape=jax.ShapeDtypeStruct(out_shape, jnp.float32),
        in_specs=[pl.BlockSpec(memory_space=pltpu.SMEM)] + [vmem] * len(arrays),
        out_specs=vmem,
        scratch_shapes=best
        + [pltpu.VMEM((rows, LANES), jnp.int32), pltpu.VMEM((rows, LANES), jnp.float32)],
        compiler_params=pltpu.CompilerParams(vmem_limit_bytes=48 * 2**20),
        name=name,
    )(where, *arrays)


def unpack_kernel(where_ref, clu_ref, spot_ref, near_ref, far_ref, out_ref):
    half = near_ref.shape[0]
    rows = clu_ref.shape[1]
    slot, _ = slot_of(clu_ref[...], where_ref[1], half)
    hot = (iota((2 * half, rows), 0) == slot).astype(jnp.bfloat16)
    total = jnp.zeros((LANES, rows), jnp.float32)
    for piece in split3(jnp.concatenate([near_ref[...], far_ref[...]], axis=0)):
        total = total + dot(piece, hot, ((0,), (0,)))
    mine = iota((LANES, rows), 0) == spot_ref[...]
    out_ref[...] = jnp.sum(jnp.where(mine, total, 0.0), axis=0, keepdims=True)


def unpack(where, clusters, spot, near, far):
    rows = clusters.shape[0]
    vmem = pl.BlockSpec(memory_space=pltpu.VMEM)
    return pl.pallas_call(
        unpack_kernel,
        out_shape=jax.ShapeDtypeStruct((1, rows), jnp.float32),
        in_specs=[pl.BlockSpec(memory_space=pltpu.SMEM)] + [vmem] * 4,
        out_specs=vmem,
        name="unpack",
    )(where, clusters.reshape(1, rows), spot, near, far).reshape(rows)


AXES = ("dp", "help")
NY, NZ, NX = 4, 8, 4


def device(y, z, core, x):
    return ((y % NY * NZ + z % NZ) * 2 + core) * NX + x % NX


EVERY = [(y, z, c, x) for y in range(NY) for z in range(NZ) for c in range(2) for x in range(NX)]
SWAP = [(device(y, z, c, x), device(y, z, 1 - c, x)) for y, z, c, x in EVERY]
GROUPS = [[device(y, z, 0, x) for y in range(NY) for z in range(NZ)] for x in range(NX)] + [
    [device(y, z, 1, x) for z in range(NZ) for x in range(NX)] for y in range(NY)
]


def aside(step):
    return [
        (device(y, z, c, x), device(y, z, c, x + step) if c == 0 else device(y + step, z, c, x))
        for y, z, c, x in EVERY
    ]


def exchange(array):
    return lax.all_to_all(
        array, AXES, split_axis=0, concat_axis=0, axis_index_groups=GROUPS, tiled=True
    )


def shards(embeddings, clusters, send_order):
    rows, depth = embeddings.shape
    owners = lax.axis_size("dp")
    half = owners // 2
    width = rows // owners
    dp, x = lax.axis_index("dp"), lax.axis_index("help")
    core, y = dp % 2, dp // (2 * NZ)
    where = jnp.stack([jnp.where(core == 0, x, y), core, jnp.int32(NX)])
    keep, send, keep_lab, send_lab, spot = pack(where, embeddings, clusters, owners)
    got, got_lab = lax.ppermute(send, AXES, SWAP), lax.ppermute(send_lab, AXES, SWAP)
    outgoing = jnp.concatenate(
        [keep.reshape(half, width, depth), got.reshape(half, width, depth)], axis=1
    )
    own = exchange(outgoing).reshape(rows, depth)
    lab = exchange((keep_lab + got_lab).reshape(half, 1, LANES)).reshape(half, LANES)
    left, right = lax.ppermute(own, AXES, aside(1)), lax.ppermute(own, AXES, aside(-1))
    lab_left, lab_right = lax.ppermute(lab, AXES, aside(1)), lax.ppermute(lab, AXES, aside(-1))
    alone = sims_call(alone_kernel, "alone", (1, rows), where, (own, lab), rows, False)
    arrays = (left, right, lab_left, lab_right)
    cross = sims_call(cross_kernel, "cross", (half, LANES), where, arrays, rows, True)
    cross = lax.ppermute(cross, AXES, aside(1))
    arrays = (alone, own, left, right, lab, lab_left, lab_right)
    best = sims_call(sides_kernel, "sides", (half, LANES), where, arrays, rows, True)
    best = jnp.maximum(best, cross)
    near = exchange(best.reshape(half, 1, LANES)).reshape(half, LANES)
    far = lax.ppermute(near, AXES, SWAP)
    return unpack(where, clusters, spot, near, far)


def solution(mesh):
    return jax.shard_map(
        shards,
        mesh=mesh,
        in_specs=(P(("dp", "help"), None), P(("dp", "help")), P(("dp", "help"))),
        out_specs=P(("dp", "help")),
        check_vma=False,
    )
```

```python
import jax
import jax.numpy as jnp
from jax import lax
from jax.experimental import pallas as pl
from jax.experimental.pallas import tpu as pltpu
from jax.sharding import PartitionSpec as P

LANES = 128
TILE = 256


def split3(x):
    high = x.astype(jnp.bfloat16)
    rest = x - high.astype(jnp.float32)
    mid = rest.astype(jnp.bfloat16)
    low = (rest - mid.astype(jnp.float32)).astype(jnp.bfloat16)
    return high, mid, low


def iota(shape, dim):
    return lax.broadcasted_iota(jnp.int32, shape, dim)


def dot(a, b, dims):
    return lax.dot_general(a, b, (dims, ((), ())), preferred_element_type=jnp.float32)


BITS = 4096.0
CHUNKS = 4


def slot_of(clusters, core, half):
    owner = clusters // 2
    away = jnp.where(owner // half == core, 0, 1)
    return owner % half + away * half, away


def pack_kernel(where_ref, emb_ref, clu_ref, keep_ref, send_ref, lab_ref, spot_ref, raw_ref, unit_ref, sems):
    rows = emb_ref.shape[0]
    devices = lab_ref.shape[0]
    step = rows // CHUNKS
    copies = [
        pltpu.make_async_copy(
            emb_ref.at[pl.ds(i * step, step)], raw_ref.at[pl.ds(i * step, step)], sems.at[i]
        )
        for i in range(CHUNKS)
    ]
    for copy in copies:
        copy.start()
    half = keep_ref.shape[0] // 16
    width = keep_ref.shape[0] // half
    clusters = clu_ref[...]
    slot, away = slot_of(clusters, where_ref[1], half)
    hot = (iota((2 * half, rows), 0) == slot).astype(jnp.bfloat16)
    before = (iota((rows, rows), 0) < iota((rows, rows), 1)).astype(jnp.bfloat16)
    count = dot(hot, before, ((1,), (0,)))
    rank = jnp.sum(hot.astype(jnp.float32) * count, axis=0, keepdims=True).astype(jnp.int32)
    spot_ref[...] = rank + away * width
    place = slot * width + rank
    bit = (clusters % 2).astype(jnp.float32)
    spots = jnp.where(iota((LANES, rows), 0) == rank, bit, 0.0).astype(jnp.bfloat16)
    target = iota((devices, rows), 0)
    line, last = target // 8, target % 4
    owner = jnp.where(target // 4 % 2 == 0, line, half + line % 8 * 4 + last)
    lab_ref[...] = dot((owner == clusters // 2).astype(jnp.bfloat16), spots, ((1,), (1,)))
    for i, copy in enumerate(copies):
        copy.wait()
        values = raw_ref[i * step : (i + 1) * step, :].astype(jnp.float32)
        scale = lax.rsqrt(jnp.sum(values * values, axis=1, keepdims=True) + 1e-06)
        unit_ref[i * step : (i + 1) * step, :] = (values * scale).astype(jnp.bfloat16)
    for out_ref, base in ((send_ref, rows // 2), (keep_ref, 0)):
        for start in range(0, rows // 2, TILE):
            pick = (iota((TILE, rows), 0) + (base + start) == place).astype(jnp.bfloat16)
            out_ref[start : start + TILE, :] = dot(pick, unit_ref[...], ((1,), (0,))).astype(
                jnp.bfloat16
            )


def smem():
    return pl.BlockSpec(memory_space=pltpu.SMEM)


def vmem():
    return pl.BlockSpec(memory_space=pltpu.VMEM)


def params():
    return pltpu.CompilerParams(vmem_limit_bytes=48 * 2**20)


def pack(where, embeddings, clusters, devices):
    rows, depth = embeddings.shape
    return pl.pallas_call(
        pack_kernel,
        out_shape=(
            jax.ShapeDtypeStruct((rows // 2, depth), jnp.bfloat16),
            jax.ShapeDtypeStruct((rows // 2, depth), jnp.bfloat16),
            jax.ShapeDtypeStruct((devices, LANES), jnp.float32),
            jax.ShapeDtypeStruct((1, rows), jnp.int32),
        ),
        in_specs=[smem(), pl.BlockSpec(memory_space=pl.ANY), vmem()],
        scratch_shapes=[
            pltpu.VMEM((rows, depth), jnp.bfloat16),
            pltpu.VMEM((rows, depth), jnp.bfloat16),
            pltpu.SemaphoreType.DMA((CHUNKS,)),
        ],
        compiler_params=params(),
        name="pack",
    )(where, embeddings, clusters.reshape(1, rows))


def order_of(place, core, part):
    source, flip, rank = place // 32, place // 16 % 2, place % 16
    from_core = jnp.where(flip == 0, core, 1 - core)
    by_row = (source * 2 + from_core) * 4 + part
    by_column = ((part * 8 + source // 4) * 2 + from_core) * 4 + source % 4
    return jnp.where(core == 0, by_row, by_column) * 16 + rank


def row_codes(lab, rows, core, part):
    devices = lab.shape[0]
    order = order_of(iota((1, rows), 1), core, part)
    hot = (iota((devices, rows), 0) == order // 16).astype(jnp.bfloat16)
    spread = dot(lab[:, :16], hot, ((0,), (0,)))
    label = jnp.sum(jnp.where(iota((16, rows), 0) == order % 16, spread, 0.0), axis=0, keepdims=True)
    return label * BITS, label * BITS + order.astype(jnp.float32)


def column_codes(lab, rows, core, part):
    devices = lab.shape[0]
    order = order_of(iota((rows, 1), 0), core, part)
    hot = (iota((rows, devices), 1) == order // 16).astype(jnp.bfloat16)
    spread = dot(hot, lab, ((1,), (0,)))
    kept = jnp.where(iota((rows, LANES), 1) == order % 16, spread, 0.0).astype(jnp.bfloat16)
    label = dot(kept, jnp.ones((LANES, LANES), jnp.bfloat16), ((1,), (0,)))
    return label * BITS + order.astype(jnp.float32)


def scan(best_ref, query_ref, key_ref, floor, ceiling, codes_ref, pick):
    rows = query_ref.shape[0]
    for start in range(0, rows, TILE):
        queries = query_ref[start : start + TILE, :]
        here = slice(start, start + TILE)
        best = best_ref[:, here]
        for low in range(0, rows, TILE):
            if not pick(low, start):
                continue
            sims = dot(key_ref[low : low + TILE, :], queries, ((1,), (1,)))
            codes = jnp.concatenate([codes_ref[low : low + TILE, :]] * (TILE // LANES), axis=1)
            mask = (codes >= floor[:, here]) & (codes < ceiling[:, here])
            found = jnp.max(jnp.where(mask, sims, -1.0), axis=0, keepdims=True)
            best = jnp.maximum(best, found)
        best_ref[:, here] = best


def scan_pair(best_ref, query_ref, key_ref, floor, ceiling, codes_ref, core, part, key_part):
    args = (best_ref, query_ref, key_ref, floor, ceiling, codes_ref)

    @pl.when((core == 0) | (key_part < part))
    def _():
        scan(*args, lambda low, start: low <= start)

    @pl.when((core != 0) & (key_part < part))
    def _():
        scan(*args, lambda low, start: low > start)


def store_groups(out_ref, best):
    sources = out_ref.shape[0]
    rows = best.shape[1]
    width = rows // sources
    mine = iota((sources, rows), 0) == iota((sources, rows), 1) // width
    spots = (iota((rows, LANES), 0) % width == iota((rows, LANES), 1)).astype(jnp.bfloat16)
    total = jnp.zeros((sources, LANES), jnp.float32)
    for piece in split3(best):
        spread = jnp.where(mine, piece.astype(jnp.float32), 0.0).astype(jnp.bfloat16)
        total = total + dot(spread, spots, ((1,), (0,)))
    out_ref[...] = total


def parts_of(where_ref):
    me, core, parts = where_ref[0], where_ref[1], where_ref[2]
    return core, me, lax.rem(me + parts - 1, parts), lax.rem(me + 1, parts)


def alone_kernel(where_ref, own_ref, lab_ref, best_ref, rows_ref, left_ref, right_ref, codes_ref):
    rows = own_ref.shape[0]
    core, me, left, right = parts_of(where_ref)
    lab = lab_ref[...].astype(jnp.bfloat16)
    floor, ceiling = row_codes(lab, rows, core, me)
    side_floor, side_ceiling = row_codes(lab, rows, core, right)
    rows_ref[...] = jnp.concatenate([floor, ceiling, side_floor, side_ceiling] * 2, axis=0)
    left_ref[...] = column_codes(lab, rows, core, left)
    right_ref[...] = column_codes(lab, rows, core, right)
    codes_ref[...] = column_codes(lab, rows, core, me)
    best_ref[...] = jnp.full((1, rows), -1.0, jnp.float32)
    scan(best_ref, own_ref, own_ref, floor, ceiling, codes_ref, lambda low, start: low <= start)


def alone(where, own, lab):
    rows = own.shape[0]
    return pl.pallas_call(
        alone_kernel,
        out_shape=(
            jax.ShapeDtypeStruct((1, rows), jnp.float32),
            jax.ShapeDtypeStruct((8, rows), jnp.float32),
            jax.ShapeDtypeStruct((rows, LANES), jnp.float32),
            jax.ShapeDtypeStruct((rows, LANES), jnp.float32),
        ),
        in_specs=[smem(), vmem(), vmem()],
        out_specs=(vmem(),) * 4,
        scratch_shapes=[pltpu.VMEM((rows, LANES), jnp.float32)],
        compiler_params=params(),
        cost_estimate=pl.CostEstimate(flops=2 * 10**9, bytes_accessed=4 * 10**6, transcendentals=0),
        name="alone",
    )(where, own, lab)


def cross_kernel(where_ref, left_ref, right_ref, rows_ref, left_codes_ref, out_ref, best_ref):
    rows = left_ref.shape[0]
    core, _, left, right = parts_of(where_ref)
    best_ref[...] = jnp.full((1, rows), -1.0, jnp.float32)
    scan_pair(
        best_ref, right_ref, left_ref, rows_ref[2:3, :], rows_ref[3:4, :], left_codes_ref, core, right, left
    )
    store_groups(out_ref, best_ref[...])


def sides_kernel(
    where_ref, alone_ref, own_ref, left_ref, right_ref, rows_ref, left_codes_ref, right_codes_ref,
    out_ref, best_ref,
):
    core, me, left, right = parts_of(where_ref)
    best_ref[...] = alone_ref[...]
    for key_ref, codes_ref, part in ((left_ref, left_codes_ref, left), (right_ref, right_codes_ref, right)):
        scan_pair(
            best_ref, own_ref, key_ref, rows_ref[0:1, :], rows_ref[1:2, :], codes_ref, core, me, part
        )
    store_groups(out_ref, best_ref[...])


def sims_call(kernel, name, groups, where, arrays, rows):
    return pl.pallas_call(
        kernel,
        out_shape=jax.ShapeDtypeStruct((groups, LANES), jnp.float32),
        in_specs=[smem()] + [vmem()] * len(arrays),
        out_specs=vmem(),
        scratch_shapes=[pltpu.VMEM((1, rows), jnp.float32)],
        compiler_params=params(),
        name=name,
    )(where, *arrays)


def unpack_kernel(where_ref, clu_ref, spot_ref, near_ref, far_ref, out_ref):
    half = near_ref.shape[0]
    rows = clu_ref.shape[1]
    slot, _ = slot_of(clu_ref[...], where_ref[1], half)
    hot = (iota((2 * half, rows), 0) == slot).astype(jnp.bfloat16)
    results = jnp.concatenate([near_ref[:, :32], far_ref[:, :32]], axis=0)
    total = jnp.zeros((32, rows), jnp.float32)
    for piece in split3(results):
        total = total + dot(piece, hot, ((0,), (0,)))
    mine = iota((32, rows), 0) == spot_ref[...]
    out_ref[...] = jnp.sum(jnp.where(mine, total, 0.0), axis=0, keepdims=True)


def unpack(where, clusters, spot, near, far):
    rows = clusters.shape[0]
    return pl.pallas_call(
        unpack_kernel,
        out_shape=jax.ShapeDtypeStruct((1, rows), jnp.float32),
        in_specs=[smem()] + [vmem()] * 4,
        out_specs=vmem(),
        name="unpack",
    )(where, clusters.reshape(1, rows), spot, near, far).reshape(rows)


AXES = ("dp", "help")
NY, NZ, NX = 4, 8, 4


def device(y, z, core, x):
    return ((y % NY * NZ + z % NZ) * 2 + core) * NX + x % NX


EVERY = [(y, z, c, x) for y in range(NY) for z in range(NZ) for c in range(2) for x in range(NX)]
SWAP = [(device(y, z, c, x), device(y, z, 1 - c, x)) for y, z, c, x in EVERY]
GROUPS = [[device(y, z, 0, x) for y in range(NY) for z in range(NZ)] for x in range(NX)] + [
    [device(y, z, 1, x) for z in range(NZ) for x in range(NX)] for y in range(NY)
]


def aside(step):
    return [
        (device(y, z, c, x), device(y, z, c, x + step) if c == 0 else device(y + step, z, c, x))
        for y, z, c, x in EVERY
    ]


def exchange(array):
    return lax.all_to_all(
        array, AXES, split_axis=0, concat_axis=0, axis_index_groups=GROUPS, tiled=True
    )


def shards(embeddings, clusters, send_order):
    rows, depth = embeddings.shape
    owners, helpers = lax.axis_size("dp"), lax.axis_size("help")
    half = owners // 2
    width = rows // owners
    devices = owners * helpers
    dp, x = lax.axis_index("dp"), lax.axis_index("help")
    core, y = dp % 2, dp // (2 * NZ)
    where = jnp.stack([jnp.where(core == 0, x, y), core, jnp.int32(NX)])
    keep, send, labels, spot = pack(where, embeddings, clusters, devices)
    got = lax.ppermute(send, AXES, SWAP)
    outgoing = jnp.concatenate(
        [keep.reshape(half, width, depth), got.reshape(half, width, depth)], axis=1
    )
    own = exchange(outgoing).reshape(rows, depth)
    left, right = lax.ppermute(own, AXES, aside(1)), lax.ppermute(own, AXES, aside(-1))
    labels = lax.all_to_all(
        labels.reshape(devices, 1, LANES), AXES, split_axis=0, concat_axis=0, tiled=True
    ).reshape(devices, LANES)
    best, codes, left_codes, right_codes = alone(where, own, labels)
    arrays = (left, right, codes, left_codes)
    cross = sims_call(cross_kernel, "cross", half, where, arrays, rows)
    cross = lax.ppermute(cross, AXES, aside(1))
    arrays = (best, own, left, right, codes, left_codes, right_codes)
    best = sims_call(sides_kernel, "sides", half, where, arrays, rows)
    best = jnp.maximum(best, cross)
    near = exchange(best.reshape(half, 1, LANES)).reshape(half, LANES)
    far = lax.ppermute(near, AXES, SWAP)
    return unpack(where, clusters, spot, near, far)


def solution(mesh):
    return jax.shard_map(
        shards,
        mesh=mesh,
        in_specs=(P(("dp", "help"), None), P(("dp", "help")), P(("dp", "help"))),
        out_specs=P(("dp", "help")),
        check_vma=False,
    )
```

```python
import jax
import jax.numpy as jnp
from jax import lax
from jax.experimental import pallas as pl
from jax.experimental.pallas import tpu as pltpu
from jax.sharding import PartitionSpec as P

LANES = 128
TILE = 256


def split3(x):
    high = x.astype(jnp.bfloat16)
    rest = x - high.astype(jnp.float32)
    mid = rest.astype(jnp.bfloat16)
    low = (rest - mid.astype(jnp.float32)).astype(jnp.bfloat16)
    return high, mid, low


def iota(shape, dim):
    return lax.broadcasted_iota(jnp.int32, shape, dim)


def dot(a, b, dims):
    return lax.dot_general(a, b, (dims, ((), ())), preferred_element_type=jnp.float32)


BITS = 4096.0
CHUNKS = 4


def slot_of(clusters, core, half):
    owner = clusters // 2
    away = jnp.where(owner // half == core, 0, 1)
    return owner % half + away * half, away


def pack_kernel(
    where_ref, emb_ref, clu_ref, keep_ref, send_ref, keep_lab_ref, send_lab_ref, spot_ref, raw_ref, unit_ref, sems
):
    rows = emb_ref.shape[0]
    step = rows // CHUNKS
    copies = [
        pltpu.make_async_copy(
            emb_ref.at[pl.ds(i * step, step)], raw_ref.at[pl.ds(i * step, step)], sems.at[i]
        )
        for i in range(CHUNKS)
    ]
    for copy in copies:
        copy.start()
    half = keep_lab_ref.shape[0]
    width = keep_ref.shape[0] // half
    clusters = clu_ref[...]
    slot, away = slot_of(clusters, where_ref[1], half)
    hot = (iota((2 * half, rows), 0) == slot).astype(jnp.bfloat16)
    before = (iota((rows, rows), 0) < iota((rows, rows), 1)).astype(jnp.bfloat16)
    count = dot(hot, before, ((1,), (0,)))
    rank = jnp.sum(hot.astype(jnp.float32) * count, axis=0, keepdims=True).astype(jnp.int32)
    spot = rank + away * width
    spot_ref[...] = spot
    place = slot * width + rank
    bit = (clusters % 2).astype(jnp.float32)
    spots = jnp.where(iota((LANES, rows), 0) == spot, bit, 0.0).astype(jnp.bfloat16)
    labels = dot(hot, spots, ((1,), (1,)))
    keep_lab_ref[...] = labels[:half]
    send_lab_ref[...] = labels[half:]
    for i, copy in enumerate(copies):
        copy.wait()
        values = raw_ref[i * step : (i + 1) * step, :].astype(jnp.float32)
        scale = lax.rsqrt(jnp.sum(values * values, axis=1, keepdims=True) + 1e-06)
        unit_ref[i * step : (i + 1) * step, :] = (values * scale).astype(jnp.bfloat16)
    for out_ref, base in ((send_ref, rows // 2), (keep_ref, 0)):
        for start in range(0, rows // 2, TILE):
            pick = (iota((TILE, rows), 0) + (base + start) == place).astype(jnp.bfloat16)
            out_ref[start : start + TILE, :] = dot(pick, unit_ref[...], ((1,), (0,))).astype(
                jnp.bfloat16
            )


def smem():
    return pl.BlockSpec(memory_space=pltpu.SMEM)


def vmem():
    return pl.BlockSpec(memory_space=pltpu.VMEM)


def params(size=48):
    return pltpu.CompilerParams(vmem_limit_bytes=size * 2**20)


def pack(where, embeddings, clusters, half):
    rows, depth = embeddings.shape
    return pl.pallas_call(
        pack_kernel,
        out_shape=(
            jax.ShapeDtypeStruct((rows // 2, depth), jnp.bfloat16),
            jax.ShapeDtypeStruct((rows // 2, depth), jnp.bfloat16),
            jax.ShapeDtypeStruct((half, LANES), jnp.float32),
            jax.ShapeDtypeStruct((half, LANES), jnp.float32),
            jax.ShapeDtypeStruct((1, rows), jnp.int32),
        ),
        in_specs=[smem(), pl.BlockSpec(memory_space=pl.ANY), vmem()],
        scratch_shapes=[
            pltpu.VMEM((rows, depth), jnp.bfloat16),
            pltpu.VMEM((rows, depth), jnp.bfloat16),
            pltpu.SemaphoreType.DMA((CHUNKS,)),
        ],
        compiler_params=params(60),
        name="pack",
    )(where, embeddings, clusters.reshape(1, rows))


def order_of(place, core, part):
    source, flip, rank = place // 32, place // 16 % 2, place % 16
    from_core = jnp.where(flip == 0, core, 1 - core)
    by_row = (source * 2 + from_core) * 4 + part
    by_column = ((part * 8 + source // 4) * 2 + from_core) * 4 + source % 4
    return jnp.where(core == 0, by_row, by_column) * 16 + rank


def row_codes(lab, rows, core, part):
    sources = lab.shape[0]
    width = rows // sources
    place = iota((1, rows), 1)
    hot = (iota((sources, rows), 0) == place // width).astype(jnp.bfloat16)
    spread = dot(lab[:, :width], hot, ((0,), (0,)))
    chosen = iota((width, rows), 0) == place % width
    label = jnp.sum(jnp.where(chosen, spread, 0.0), axis=0, keepdims=True)
    return label * BITS, label * BITS + order_of(place, core, part).astype(jnp.float32)


def column_codes(lab, rows, core, part):
    sources = lab.shape[0]
    width = rows // sources
    place = iota((rows, 1), 0)
    hot = (iota((rows, sources), 1) == place // width).astype(jnp.bfloat16)
    spread = dot(hot, lab, ((1,), (0,)))
    chosen = iota((rows, LANES), 1) == place % width
    kept = jnp.where(chosen, spread, 0.0).astype(jnp.bfloat16)
    label = dot(kept, jnp.ones((LANES, LANES), jnp.bfloat16), ((1,), (0,)))
    return label * BITS + order_of(iota((rows, LANES), 0), core, part).astype(jnp.float32)


def scan(best_ref, query_ref, key_ref, floor, ceiling, codes_ref, pick):
    rows = query_ref.shape[0]
    for start in range(0, rows, TILE):
        queries = query_ref[start : start + TILE, :]
        here = slice(start, start + TILE)
        best = best_ref[:, here]
        for low in range(0, rows, TILE):
            if not pick(low, start):
                continue
            sims = dot(key_ref[low : low + TILE, :], queries, ((1,), (1,)))
            codes = jnp.concatenate([codes_ref[low : low + TILE, :]] * (TILE // LANES), axis=1)
            mask = (codes >= floor[:, here]) & (codes < ceiling[:, here])
            found = jnp.max(jnp.where(mask, sims, -1.0), axis=0, keepdims=True)
            best = jnp.maximum(best, found)
        best_ref[:, here] = best


def scan_pair(best_ref, query_ref, key_ref, floor, ceiling, codes_ref, core, part, key_part):
    args = (best_ref, query_ref, key_ref, floor, ceiling, codes_ref)

    @pl.when((core == 0) | (key_part < part))
    def _():
        scan(*args, lambda low, start: low <= start)

    @pl.when((core != 0) & (key_part < part))
    def _():
        scan(*args, lambda low, start: low > start)


def store_groups(out_ref, best):
    sources = out_ref.shape[0]
    rows = best.shape[1]
    width = rows // sources
    mine = iota((sources, rows), 0) == iota((sources, rows), 1) // width
    spots = (iota((rows, LANES), 0) % width == iota((rows, LANES), 1)).astype(jnp.bfloat16)
    total = jnp.zeros((sources, LANES), jnp.float32)
    for piece in split3(best):
        spread = jnp.where(mine, piece.astype(jnp.float32), 0.0).astype(jnp.bfloat16)
        total = total + dot(spread, spots, ((1,), (0,)))
    out_ref[...] = total


def parts_of(where_ref):
    me, core, parts = where_ref[0], where_ref[1], where_ref[2]
    return core, me, lax.rem(me + parts - 1, parts), lax.rem(me + 1, parts)


def alone_kernel(where_ref, own_ref, lab_ref, best_ref, rows_ref, left_ref, right_ref, codes_ref):
    rows = own_ref.shape[0]
    core, me, left, right = parts_of(where_ref)
    lab, left_lab, right_lab = (lab_ref[:, i, :].astype(jnp.bfloat16) for i in range(3))
    floor, ceiling = row_codes(lab, rows, core, me)
    side_floor, side_ceiling = row_codes(right_lab, rows, core, right)
    rows_ref[...] = jnp.concatenate([floor, ceiling, side_floor, side_ceiling] * 2, axis=0)
    left_ref[...] = column_codes(left_lab, rows, core, left)
    right_ref[...] = column_codes(right_lab, rows, core, right)
    codes_ref[...] = column_codes(lab, rows, core, me)
    best_ref[...] = jnp.full((1, rows), -1.0, jnp.float32)
    scan(best_ref, own_ref, own_ref, floor, ceiling, codes_ref, lambda low, start: low <= start)


def alone(where, own, lab):
    rows = own.shape[0]
    return pl.pallas_call(
        alone_kernel,
        out_shape=(
            jax.ShapeDtypeStruct((1, rows), jnp.float32),
            jax.ShapeDtypeStruct((8, rows), jnp.float32),
            jax.ShapeDtypeStruct((rows, LANES), jnp.float32),
            jax.ShapeDtypeStruct((rows, LANES), jnp.float32),
        ),
        in_specs=[smem(), vmem(), vmem()],
        out_specs=(vmem(),) * 4,
        scratch_shapes=[pltpu.VMEM((rows, LANES), jnp.float32)],
        compiler_params=params(),
        cost_estimate=pl.CostEstimate(flops=2 * 10**9, bytes_accessed=4 * 10**6, transcendentals=0),
        name="alone",
    )(where, own, lab)


def cross_kernel(where_ref, left_ref, right_ref, rows_ref, left_codes_ref, out_ref, best_ref):
    rows = left_ref.shape[0]
    core, _, left, right = parts_of(where_ref)
    best_ref[...] = jnp.full((1, rows), -1.0, jnp.float32)
    scan_pair(
        best_ref, right_ref, left_ref, rows_ref[2:3, :], rows_ref[3:4, :], left_codes_ref, core, right, left
    )
    store_groups(out_ref, best_ref[...])


def sides_kernel(
    where_ref, alone_ref, own_ref, left_ref, right_ref, rows_ref, left_codes_ref, right_codes_ref,
    out_ref, best_ref,
):
    core, me, left, right = parts_of(where_ref)
    best_ref[...] = alone_ref[...]
    for key_ref, codes_ref, part in ((left_ref, left_codes_ref, left), (right_ref, right_codes_ref, right)):
        scan_pair(
            best_ref, own_ref, key_ref, rows_ref[0:1, :], rows_ref[1:2, :], codes_ref, core, me, part
        )
    store_groups(out_ref, best_ref[...])


def sims_call(kernel, name, groups, where, arrays, rows):
    return pl.pallas_call(
        kernel,
        out_shape=jax.ShapeDtypeStruct((groups, LANES), jnp.float32),
        in_specs=[smem()] + [vmem()] * len(arrays),
        out_specs=vmem(),
        scratch_shapes=[pltpu.VMEM((1, rows), jnp.float32)],
        compiler_params=params(),
        name=name,
    )(where, *arrays)


def unpack_kernel(where_ref, clu_ref, spot_ref, near_ref, far_ref, out_ref):
    half = near_ref.shape[0]
    rows = clu_ref.shape[1]
    slot, _ = slot_of(clu_ref[...], where_ref[1], half)
    hot = (iota((2 * half, rows), 0) == slot).astype(jnp.bfloat16)
    results = jnp.concatenate([near_ref[:, :32], far_ref[:, :32]], axis=0)
    total = jnp.zeros((32, rows), jnp.float32)
    for piece in split3(results):
        total = total + dot(piece, hot, ((0,), (0,)))
    mine = iota((32, rows), 0) == spot_ref[...]
    out_ref[...] = jnp.sum(jnp.where(mine, total, 0.0), axis=0, keepdims=True)


def unpack(where, clusters, spot, near, far):
    rows = clusters.shape[0]
    return pl.pallas_call(
        unpack_kernel,
        out_shape=jax.ShapeDtypeStruct((1, rows), jnp.float32),
        in_specs=[smem()] + [vmem()] * 4,
        out_specs=vmem(),
        name="unpack",
    )(where, clusters.reshape(1, rows), spot, near, far).reshape(rows)


AXES = ("dp", "help")
NY, NZ, NX = 4, 8, 4


def device(y, z, core, x):
    return ((y % NY * NZ + z % NZ) * 2 + core) * NX + x % NX


EVERY = [(y, z, c, x) for y in range(NY) for z in range(NZ) for c in range(2) for x in range(NX)]
SWAP = [(device(y, z, c, x), device(y, z, 1 - c, x)) for y, z, c, x in EVERY]
GROUPS = [[device(y, z, 0, x) for y in range(NY) for z in range(NZ)] for x in range(NX)] + [
    [device(y, z, 1, x) for z in range(NZ) for x in range(NX)] for y in range(NY)
]


def aside(step):
    return [
        (device(y, z, c, x), device(y, z, c, x + step) if c == 0 else device(y + step, z, c, x))
        for y, z, c, x in EVERY
    ]


def across(step):
    return [
        (device(y, z, c, x), device(y, z, 0, x + step) if c == 1 else device(y + step, z, 1, x))
        for y, z, c, x in EVERY
    ]


def exchange(array):
    return lax.all_to_all(
        array, AXES, split_axis=0, concat_axis=0, axis_index_groups=GROUPS, tiled=True
    )


def shards(embeddings, clusters, send_order):
    rows, depth = embeddings.shape
    owners = lax.axis_size("dp")
    half = owners // 2
    width = rows // owners
    dp, x = lax.axis_index("dp"), lax.axis_index("help")
    core, y = dp % 2, dp // (2 * NZ)
    where = jnp.stack([jnp.where(core == 0, x, y), core, jnp.int32(NX)])
    keep, send, keep_lab, send_lab, spot = pack(where, embeddings, clusters, half)
    got = lax.ppermute(send, AXES, SWAP)
    labels = [keep_lab + lax.ppermute(send_lab, AXES, SWAP)]
    for step in (1, -1):
        labels.append(
            lax.ppermute(keep_lab, AXES, aside(step)) + lax.ppermute(send_lab, AXES, across(step))
        )
    labels = jnp.stack(labels + [jnp.zeros_like(keep_lab)], axis=1)
    outgoing = jnp.concatenate(
        [keep.reshape(half, width, depth), got.reshape(half, width, depth)], axis=1
    )
    outgoing, labels = lax.optimization_barrier((outgoing, labels))
    own = exchange(outgoing).reshape(rows, depth)
    left, right = lax.ppermute(own, AXES, aside(1)), lax.ppermute(own, AXES, aside(-1))
    labels = exchange(labels)
    best, codes, left_codes, right_codes = alone(where, own, labels)
    arrays = (left, right, codes, left_codes)
    cross = sims_call(cross_kernel, "cross", half, where, arrays, rows)
    cross = lax.ppermute(cross, AXES, aside(1))
    arrays = (best, own, left, right, codes, left_codes, right_codes)
    best = sims_call(sides_kernel, "sides", half, where, arrays, rows)
    best = jnp.maximum(best, cross)
    near = exchange(best.reshape(half, 1, LANES)).reshape(half, LANES)
    far = lax.ppermute(near, AXES, SWAP)
    return unpack(where, clusters, spot, near, far)


def solution(mesh):
    return jax.shard_map(
        shards,
        mesh=mesh,
        in_specs=(P(("dp", "help"), None), P(("dp", "help")), P(("dp", "help"))),
        out_specs=P(("dp", "help")),
        check_vma=False,
    )
```

```python
import jax
import jax.numpy as jnp
from jax import lax
from jax.experimental import pallas as pl
from jax.experimental.pallas import tpu as pltpu
from jax.sharding import PartitionSpec as P

LANES = 128
TILE = 256


def split3(x):
    high = x.astype(jnp.bfloat16)
    rest = x - high.astype(jnp.float32)
    mid = rest.astype(jnp.bfloat16)
    low = (rest - mid.astype(jnp.float32)).astype(jnp.bfloat16)
    return high, mid, low


def iota(shape, dim):
    return lax.broadcasted_iota(jnp.int32, shape, dim)


def dot(a, b, dims):
    return lax.dot_general(a, b, (dims, ((), ())), preferred_element_type=jnp.float32)


BITS = 4096.0
GROUP = 16
NOTE = 8


def slot_of(clusters, core, half):
    owner = clusters // 2
    away = jnp.where(owner // half == core, 0, 1)
    return owner % half + away * half, away


def smem():
    return pl.BlockSpec(memory_space=pltpu.SMEM)


def vmem():
    return pl.BlockSpec(memory_space=pltpu.VMEM)


def call(kernel, name, ins, outs, scratch=(), flops=0):
    return pl.pallas_call(
        kernel,
        out_shape=tuple(jax.ShapeDtypeStruct(shape, kind) for shape, kind in outs),
        in_specs=[smem()] + [vmem()] * (len(ins) - 1),
        out_specs=(vmem(),) * len(outs),
        scratch_shapes=[pltpu.VMEM(shape, kind) for shape, kind in scratch],
        compiler_params=pltpu.CompilerParams(vmem_limit_bytes=48 * 2**20),
        cost_estimate=pl.CostEstimate(flops=flops, bytes_accessed=2**20, transcendentals=0),
        name=name,
    )(*ins)


def put_rows(out_ref, unit_ref, place, base):
    rows = unit_ref.shape[0]
    each = TILE // GROUP
    for start in range(0, rows // 2, TILE):
        pick = (iota((TILE, rows), 0) + (base + start) == place).astype(jnp.bfloat16)
        block = dot(pick, unit_ref[...], ((1,), (0,))).astype(jnp.bfloat16)
        first = start // GROUP
        for lane in range(block.shape[1] // LANES):
            out_ref[first : first + each, lane * GROUP : (lane + 1) * GROUP, :] = block[
                :, lane * LANES : (lane + 1) * LANES
            ].reshape(each, GROUP, LANES)


def send_kernel(where_ref, emb_ref, clu_ref, send_ref, notes_ref, unit_ref, rows_ref):
    rows = emb_ref.shape[0]
    half = send_ref.shape[0]
    clusters = clu_ref[...]
    slot, away = slot_of(clusters, where_ref[1], half)
    hot = (iota((2 * half, rows), 0) == slot).astype(jnp.bfloat16)
    before = (iota((rows, rows), 0) < iota((rows, rows), 1)).astype(jnp.bfloat16)
    count = dot(hot, before, ((1,), (0,)))
    rank = jnp.sum(hot.astype(jnp.float32) * count, axis=0, keepdims=True).astype(jnp.int32)
    spot = rank + away * GROUP
    place = slot * GROUP + rank
    rows_ref[...] = jnp.concatenate([slot, spot, place, place] * 2, axis=0)
    bit = (clusters % 2).astype(jnp.float32)
    spots = jnp.where(iota((LANES, rows), 0) == spot, bit, 0.0).astype(jnp.bfloat16)
    labels = dot(hot, spots, ((1,), (1,))).astype(jnp.bfloat16)
    notes_ref[...] = jnp.broadcast_to(labels[:half, None, :], (half, NOTE, LANES))
    values = emb_ref[...].astype(jnp.float32)
    scale = lax.rsqrt(jnp.sum(values * values, axis=1, keepdims=True) + 1e-06)
    unit_ref[...] = (values * scale).astype(jnp.bfloat16)
    put_rows(send_ref, unit_ref, place, rows // 2)
    data = send_ref.shape[1] - NOTE
    send_ref[:, data:, :] = jnp.broadcast_to(labels[half:, None, :], (half, NOTE, LANES))


def keep_kernel(where_ref, unit_ref, rows_ref, keep_ref):
    put_rows(keep_ref, unit_ref, rows_ref[2:3, :], 0)


def source_of(place):
    return place // TILE * (TILE // (2 * GROUP)) + place % (TILE // 2) // GROUP


def lane_of(place):
    return place // (TILE // 2) % 2 * GROUP + place % GROUP


def order_of(place, core, part):
    source, flip, rank = source_of(place), place // (TILE // 2) % 2, place % GROUP
    from_core = jnp.where(flip == 0, core, 1 - core)
    by_row = (source * 2 + from_core) * 4 + part
    by_column = ((part * 8 + source // 4) * 2 + from_core) * 4 + source % 4
    return jnp.where(core == 0, by_row, by_column) * GROUP + rank


def tile_of(ref, index):
    each = TILE // (2 * GROUP)
    data = (ref.shape[1] - NOTE) // 2
    here = slice(index * each, (index + 1) * each)
    lanes = []
    for base in range(0, data, GROUP):
        parts = [
            ref[here, start : start + GROUP, :].reshape(TILE // 2, LANES)
            for start in (base, data + base)
        ]
        lanes.append(jnp.concatenate(parts, axis=0))
    return jnp.concatenate(lanes, axis=1)


def notes_of(ref):
    data = ref.shape[1] - NOTE
    return (jnp.sum(ref[:, data:, :].astype(jnp.float32), axis=1) * (1.0 / NOTE)).astype(jnp.bfloat16)


def row_codes(lab, rows, core, part):
    sources = lab.shape[0]
    width = 2 * GROUP
    place = iota((1, rows), 1)
    hot = (iota((sources, rows), 0) == source_of(place)).astype(jnp.bfloat16)
    spread = dot(lab[:, :width], hot, ((0,), (0,)))
    chosen = iota((width, rows), 0) == lane_of(place)
    label = jnp.sum(jnp.where(chosen, spread, 0.0), axis=0, keepdims=True)
    return label * BITS, label * BITS + order_of(place, core, part).astype(jnp.float32)


def column_codes(lab, rows, core, part):
    sources = lab.shape[0]
    place = iota((rows, 1), 0)
    hot = (iota((rows, sources), 1) == source_of(place)).astype(jnp.bfloat16)
    spread = dot(hot, lab, ((1,), (0,)))
    chosen = iota((rows, LANES), 1) == lane_of(place)
    kept = jnp.where(chosen, spread, 0.0).astype(jnp.bfloat16)
    label = dot(kept, jnp.ones((LANES, LANES), jnp.bfloat16), ((1,), (0,)))
    return label * BITS + order_of(place, core, part).astype(jnp.float32)


def scan(best_ref, query_ref, key_ref, floor, ceiling, codes_ref, pick):
    tiles = best_ref.shape[1] // TILE
    for query in range(tiles):
        queries = tile_of(query_ref, query)
        here = slice(query * TILE, (query + 1) * TILE)
        best = best_ref[:, here]
        for key in range(tiles):
            if not pick(key, query):
                continue
            sims = dot(tile_of(key_ref, key), queries, ((1,), (1,)))
            codes = codes_ref[key * TILE : (key + 1) * TILE, :]
            codes = jnp.concatenate([codes] * (TILE // LANES), axis=1)
            mask = (codes >= floor[:, here]) & (codes < ceiling[:, here])
            found = jnp.max(jnp.where(mask, sims, -1.0), axis=0, keepdims=True)
            best = jnp.maximum(best, found)
        best_ref[:, here] = best


def scan_pair(best_ref, query_ref, key_ref, floor, ceiling, codes_ref, core, part, key_part):
    args = (best_ref, query_ref, key_ref, floor, ceiling, codes_ref)

    @pl.when((core == 0) | (key_part < part))
    def _():
        scan(*args, lambda key, query: key <= query)

    @pl.when((core != 0) & (key_part < part))
    def _():
        scan(*args, lambda key, query: key > query)


def store_groups(out_ref, best):
    sources = out_ref.shape[0]
    rows = best.shape[1]
    mine = iota((sources, rows), 0) == source_of(iota((1, rows), 1))
    spots = (iota((rows, LANES), 1) == lane_of(iota((rows, 1), 0))).astype(jnp.bfloat16)
    total = jnp.zeros((sources, LANES), jnp.float32)
    for piece in split3(best):
        spread = jnp.where(mine, piece.astype(jnp.float32), 0.0).astype(jnp.bfloat16)
        total = total + dot(spread, spots, ((1,), (0,)))
    out_ref[...] = total


def parts_of(where_ref):
    me, core, parts = where_ref[0], where_ref[1], where_ref[2]
    return core, me, lax.rem(me + parts - 1, parts), lax.rem(me + 1, parts)


def alone_kernel(where_ref, own_ref, back_ref, best_ref, rows_ref, kept_ref, codes_ref):
    rows = best_ref.shape[1]
    core, me, _, _ = parts_of(where_ref)
    kept_ref[...] = back_ref[...]
    lab = notes_of(own_ref)
    floor, ceiling = row_codes(lab, rows, core, me)
    rows_ref[...] = jnp.concatenate([floor, ceiling] * 4, axis=0)
    codes_ref[...] = column_codes(lab, rows, core, me)
    best_ref[...] = jnp.full((1, rows), -1.0, jnp.float32)
    scan(best_ref, own_ref, own_ref, floor, ceiling, codes_ref, lambda key, query: key <= query)


def right_kernel(where_ref, alone_ref, own_ref, right_ref, rows_ref, best_ref, right_rows_ref, codes_ref):
    rows = best_ref.shape[1]
    core, me, _, right = parts_of(where_ref)
    best_ref[...] = alone_ref[...]
    lab = notes_of(right_ref)
    floor, ceiling = row_codes(lab, rows, core, right)
    right_rows_ref[...] = jnp.concatenate([floor, ceiling] * 4, axis=0)
    codes_ref[...] = column_codes(lab, rows, core, right)
    scan_pair(
        best_ref, own_ref, right_ref, rows_ref[0:1, :], rows_ref[1:2, :], codes_ref, core, me, right
    )


def cross_kernel(where_ref, left_ref, right_ref, rows_ref, out_ref, codes_ref, best_ref):
    rows = best_ref.shape[1]
    core, _, left, right = parts_of(where_ref)
    codes_ref[...] = column_codes(notes_of(left_ref), rows, core, left)
    best_ref[...] = jnp.full((1, rows), -1.0, jnp.float32)
    scan_pair(
        best_ref, right_ref, left_ref, rows_ref[0:1, :], rows_ref[1:2, :], codes_ref, core, right, left
    )
    store_groups(out_ref, best_ref[...])


def left_kernel(where_ref, found_ref, own_ref, left_ref, rows_ref, codes_ref, out_ref, best_ref):
    core, me, left, _ = parts_of(where_ref)
    best_ref[...] = found_ref[...]
    scan_pair(
        best_ref, own_ref, left_ref, rows_ref[0:1, :], rows_ref[1:2, :], codes_ref, core, me, left
    )
    store_groups(out_ref, best_ref[...])


def unpack_kernel(where_ref, back_ref, near_ref, far_ref, out_ref):
    half = near_ref.shape[0]
    rows = back_ref.shape[1]
    width = 2 * GROUP
    hot = (iota((2 * half, rows), 0) == back_ref[0:1, :]).astype(jnp.bfloat16)
    results = jnp.concatenate([near_ref[:, :width], far_ref[:, :width]], axis=0)
    total = jnp.zeros((width, rows), jnp.float32)
    for piece in split3(results):
        total = total + dot(piece, hot, ((0,), (0,)))
    mine = iota((width, rows), 0) == back_ref[1:2, :]
    out_ref[...] = jnp.sum(jnp.where(mine, total, 0.0), axis=0, keepdims=True)


AXES = ("dp", "help")
NY, NZ, NX = 4, 8, 4


def device(y, z, core, x):
    return ((y % NY * NZ + z % NZ) * 2 + core) * NX + x % NX


EVERY = [(y, z, c, x) for y in range(NY) for z in range(NZ) for c in range(2) for x in range(NX)]
SWAP = [(device(y, z, c, x), device(y, z, 1 - c, x)) for y, z, c, x in EVERY]
GROUPS = [[device(y, z, 0, x) for y in range(NY) for z in range(NZ)] for x in range(NX)] + [
    [device(y, z, 1, x) for z in range(NZ) for x in range(NX)] for y in range(NY)
]


def aside(step):
    return [
        (device(y, z, c, x), device(y, z, c, x + step) if c == 0 else device(y + step, z, c, x))
        for y, z, c, x in EVERY
    ]


def exchange(array):
    return lax.all_to_all(
        array, AXES, split_axis=0, concat_axis=0, axis_index_groups=GROUPS, tiled=True
    )


def shards(embeddings, clusters, send_order):
    rows, depth = embeddings.shape
    half = lax.axis_size("dp") // 2
    data = GROUP * (depth // LANES)
    dp, x = lax.axis_index("dp"), lax.axis_index("help")
    core, y = dp % 2, dp // (2 * NZ)
    where = jnp.stack([jnp.where(core == 0, x, y), core, jnp.int32(NX)])
    half_float, full_float, whole = jnp.bfloat16, jnp.float32, jnp.int32
    send, notes, unit, back = call(
        send_kernel,
        "send",
        (where, embeddings, clusters.reshape(1, rows)),
        (
            ((half, data + NOTE, LANES), half_float),
            ((half, NOTE, LANES), half_float),
            ((rows, depth), half_float),
            ((8, rows), whole),
        ),
    )
    got = lax.ppermute(send, AXES, SWAP)
    (keep,) = call(
        keep_kernel, "keep", (where, unit, back), (((half, data, LANES), half_float),), flops=10**9
    )
    outgoing = jnp.concatenate([keep, got[:, :data], notes + got[:, data:]], axis=1)
    own = exchange(outgoing)
    left, right = lax.ppermute(own, AXES, aside(1)), lax.ppermute(own, AXES, aside(-1))
    row, lines = ((1, rows), full_float), ((8, rows), full_float)
    codes, groups = ((rows, LANES), full_float), ((half, LANES), full_float)
    best, own_rows, back = call(
        alone_kernel, "alone", (where, own, back), (row, lines, ((8, rows), whole)), (codes,), 10**9
    )
    best, right_rows = call(
        right_kernel, "right", (where, best, own, right, own_rows), (row, lines), (codes,), 10**9
    )
    cross, left_codes = call(
        cross_kernel, "cross", (where, left, right, right_rows), (groups, codes), (row,), 10**9
    )
    cross = lax.ppermute(cross, AXES, aside(1))
    (best,) = call(
        left_kernel, "left", (where, best, own, left, own_rows, left_codes), (groups,), (row,), 10**9
    )
    best = jnp.maximum(best, cross)
    near = exchange(best.reshape(half, 1, LANES)).reshape(half, LANES)
    far = lax.ppermute(near, AXES, SWAP)
    (out,) = call(unpack_kernel, "unpack", (where, back, near, far), (row,))
    return out.reshape(rows)


def solution(mesh):
    return jax.shard_map(
        shards,
        mesh=mesh,
        in_specs=(P(("dp", "help"), None), P(("dp", "help")), P(("dp", "help"))),
        out_specs=P(("dp", "help")),
        check_vma=False,
    )
```

```python
import jax
import jax.numpy as jnp
from jax import lax
from jax.experimental import pallas as pl
from jax.experimental.pallas import tpu as pltpu
from jax.sharding import PartitionSpec as P

LANES = 128
TILE = 256


def split3(x):
    high = x.astype(jnp.bfloat16)
    rest = x - high.astype(jnp.float32)
    mid = rest.astype(jnp.bfloat16)
    low = (rest - mid.astype(jnp.float32)).astype(jnp.bfloat16)
    return high, mid, low


def iota(shape, dim):
    return lax.broadcasted_iota(jnp.int32, shape, dim)


def dot(a, b, dims):
    return lax.dot_general(a, b, (dims, ((), ())), preferred_element_type=jnp.float32)


BITS = 4096.0
GROUP = 16
NOTE = 8


def slot_of(clusters, core, half):
    owner = clusters // 2
    away = jnp.where(owner // half == core, 0, 1)
    return owner % half + away * half, away


def smem():
    return pl.BlockSpec(memory_space=pltpu.SMEM)


def vmem():
    return pl.BlockSpec(memory_space=pltpu.VMEM)


def call(kernel, name, ins, outs, scratch=(), flops=0):
    return pl.pallas_call(
        kernel,
        out_shape=tuple(jax.ShapeDtypeStruct(shape, kind) for shape, kind in outs),
        in_specs=[smem()] + [vmem()] * (len(ins) - 1),
        out_specs=(vmem(),) * len(outs),
        scratch_shapes=[pltpu.VMEM(shape, kind) for shape, kind in scratch],
        compiler_params=pltpu.CompilerParams(vmem_limit_bytes=48 * 2**20),
        cost_estimate=pl.CostEstimate(flops=flops, bytes_accessed=2**20, transcendentals=0),
        name=name,
    )(*ins)


def put_rows(out_ref, unit_ref, place, base):
    rows = unit_ref.shape[0]
    each = TILE // GROUP
    for start in range(0, rows // 2, TILE):
        pick = (iota((TILE, rows), 0) + (base + start) == place).astype(jnp.bfloat16)
        block = dot(pick, unit_ref[...], ((1,), (0,))).astype(jnp.bfloat16)
        first = start // GROUP
        for lane in range(block.shape[1] // LANES):
            out_ref[first : first + each, lane * GROUP : (lane + 1) * GROUP, :] = block[
                :, lane * LANES : (lane + 1) * LANES
            ].reshape(each, GROUP, LANES)


def send_kernel(where_ref, emb_ref, clu_ref, send_ref, notes_ref, unit_ref, rows_ref):
    rows = emb_ref.shape[0]
    half = send_ref.shape[0]
    clusters = clu_ref[...]
    slot, away = slot_of(clusters, where_ref[1], half)
    hot = (iota((2 * half, rows), 0) == slot).astype(jnp.bfloat16)
    before = (iota((rows, rows), 0) < iota((rows, rows), 1)).astype(jnp.bfloat16)
    count = dot(hot, before, ((1,), (0,)))
    rank = jnp.sum(hot.astype(jnp.float32) * count, axis=0, keepdims=True).astype(jnp.int32)
    spot = rank + away * GROUP
    place = slot * GROUP + rank
    rows_ref[...] = jnp.concatenate([slot, spot, place, place] * 2, axis=0)
    bit = (clusters % 2).astype(jnp.float32)
    spots = jnp.where(iota((LANES, rows), 0) == spot, bit, 0.0).astype(jnp.bfloat16)
    labels = dot(hot, spots, ((1,), (1,))).astype(jnp.bfloat16)
    notes_ref[...] = jnp.broadcast_to(labels[:half, None, :], (half, NOTE, LANES))
    values = emb_ref[...].astype(jnp.float32)
    scale = lax.rsqrt(jnp.sum(values * values, axis=1, keepdims=True) + 1e-06)
    unit_ref[...] = (values * scale).astype(jnp.bfloat16)
    put_rows(send_ref, unit_ref, place, rows // 2)
    data = send_ref.shape[1] - NOTE
    send_ref[:, data:, :] = jnp.broadcast_to(labels[half:, None, :], (half, NOTE, LANES))


def keep_kernel(where_ref, unit_ref, rows_ref, keep_ref):
    put_rows(keep_ref, unit_ref, rows_ref[2:3, :], 0)


def source_of(place):
    return place // TILE * (TILE // (2 * GROUP)) + place % (TILE // 2) // GROUP


def lane_of(place):
    return place // (TILE // 2) % 2 * GROUP + place % GROUP


def order_of(place, core, part):
    source, flip, rank = source_of(place), place // (TILE // 2) % 2, place % GROUP
    from_core = jnp.where(flip == 0, core, 1 - core)
    by_row = (source * 2 + from_core) * 4 + part
    by_column = ((part * 8 + source // 4) * 2 + from_core) * 4 + source % 4
    return jnp.where(core == 0, by_row, by_column) * GROUP + rank


def tile_of(ref, index):
    each = TILE // (2 * GROUP)
    data = (ref.shape[1] - NOTE) // 2
    here = slice(index * each, (index + 1) * each)
    lanes = []
    for base in range(0, data, GROUP):
        parts = [
            ref[here, start : start + GROUP, :].reshape(TILE // 2, LANES)
            for start in (base, data + base)
        ]
        lanes.append(jnp.concatenate(parts, axis=0))
    return jnp.concatenate(lanes, axis=1)


def notes_of(ref):
    data = ref.shape[1] - NOTE
    return (jnp.sum(ref[:, data:, :].astype(jnp.float32), axis=1) * (1.0 / NOTE)).astype(jnp.bfloat16)


def row_codes(lab, rows, core, part):
    sources = lab.shape[0]
    width = 2 * GROUP
    place = iota((1, rows), 1)
    hot = (iota((sources, rows), 0) == source_of(place)).astype(jnp.bfloat16)
    spread = dot(lab[:, :width], hot, ((0,), (0,)))
    chosen = iota((width, rows), 0) == lane_of(place)
    label = jnp.sum(jnp.where(chosen, spread, 0.0), axis=0, keepdims=True)
    return label * BITS, label * BITS + order_of(place, core, part).astype(jnp.float32)


def column_orders(rows, core, part):
    place = iota((rows, LANES), 0)
    return order_of(place, core, part).astype(jnp.float32)


def column_codes(lab, orders):
    rows = orders.shape[0]
    sources = lab.shape[0]
    place = iota((rows, 1), 0)
    hot = (iota((rows, sources), 1) == source_of(place)).astype(jnp.bfloat16)
    spread = dot(hot, lab, ((1,), (0,)))
    chosen = iota((rows, LANES), 1) == lane_of(place)
    kept = jnp.where(chosen, spread, 0.0).astype(jnp.bfloat16)
    label = dot(kept, jnp.ones((LANES, LANES), jnp.bfloat16), ((1,), (0,)))
    return label * BITS + orders


def scan(best_ref, query_ref, key_ref, floor, ceiling, codes_ref, pick):
    tiles = best_ref.shape[1] // TILE
    for query in range(tiles):
        queries = tile_of(query_ref, query)
        here = slice(query * TILE, (query + 1) * TILE)
        best = best_ref[:, here]
        for key in range(tiles):
            if not pick(key, query):
                continue
            sims = dot(tile_of(key_ref, key), queries, ((1,), (1,)))
            codes = codes_ref[key * TILE : (key + 1) * TILE, :]
            codes = jnp.concatenate([codes] * (TILE // LANES), axis=1)
            mask = (codes >= floor[:, here]) & (codes < ceiling[:, here])
            found = jnp.max(jnp.where(mask, sims, -1.0), axis=0, keepdims=True)
            best = jnp.maximum(best, found)
        best_ref[:, here] = best


def scan_pair(best_ref, query_ref, key_ref, floor, ceiling, codes_ref, core, part, key_part):
    args = (best_ref, query_ref, key_ref, floor, ceiling, codes_ref)

    @pl.when((core == 0) | (key_part < part))
    def _():
        scan(*args, lambda key, query: key <= query)

    @pl.when((core != 0) & (key_part < part))
    def _():
        scan(*args, lambda key, query: key > query)


def grouped(best, sources, shift):
    rows = best.shape[1]
    mine = iota((sources, rows), 0) == source_of(iota((1, rows), 1))
    spots = iota((rows, LANES), 1) == lane_of(iota((rows, 1), 0)) + shift
    pieces = [jnp.where(mine, piece.astype(jnp.float32), 0.0) for piece in split3(best)]
    spread = jnp.concatenate(pieces, axis=0).astype(jnp.bfloat16)
    total = dot(spread, spots.astype(jnp.bfloat16), ((1,), (0,)))
    return total[:sources] + total[sources : 2 * sources] + total[2 * sources :]


def parts_of(where_ref):
    me, core, parts = where_ref[0], where_ref[1], where_ref[2]
    return core, me, lax.rem(me + parts - 1, parts), lax.rem(me + 1, parts)


def alone_kernel(where_ref, own_ref, back_ref, best_ref, rows_ref, kept_ref, codes_ref):
    rows = best_ref.shape[1]
    core, me, _, _ = parts_of(where_ref)
    kept_ref[...] = back_ref[...]
    lab = notes_of(own_ref)
    floor, ceiling = row_codes(lab, rows, core, me)
    rows_ref[...] = jnp.concatenate([floor, ceiling] * 4, axis=0)
    codes_ref[...] = column_codes(lab, column_orders(rows, core, me))
    best_ref[...] = jnp.full((1, rows), -1.0, jnp.float32)
    scan(best_ref, own_ref, own_ref, floor, ceiling, codes_ref, lambda key, query: key <= query)


def right_kernel(
    where_ref, alone_ref, own_ref, right_ref, rows_ref, best_ref, right_rows_ref, orders_ref, codes_ref
):
    rows = best_ref.shape[1]
    core, me, left, right = parts_of(where_ref)
    best_ref[...] = alone_ref[...]
    lab = notes_of(right_ref)
    floor, ceiling = row_codes(lab, rows, core, right)
    right_rows_ref[...] = jnp.concatenate([floor, ceiling] * 4, axis=0)
    orders_ref[...] = column_orders(rows, core, left)
    codes_ref[...] = column_codes(lab, column_orders(rows, core, right))
    scan_pair(
        best_ref, own_ref, right_ref, rows_ref[0:1, :], rows_ref[1:2, :], codes_ref, core, me, right
    )


def left_kernel(
    where_ref, found_ref, own_ref, left_ref, right_ref, rows_ref, right_rows_ref, orders_ref,
    out_ref, best_ref, cross_ref, codes_ref,
):
    rows = best_ref.shape[1]
    core, me, left, right = parts_of(where_ref)
    best_ref[...] = found_ref[...]
    cross_ref[...] = jnp.full((1, rows), -1.0, jnp.float32)
    codes_ref[...] = column_codes(notes_of(left_ref), orders_ref[...])
    for bests, query_ref, lines_ref, part in (
        (best_ref, own_ref, rows_ref, me),
        (cross_ref, right_ref, right_rows_ref, right),
    ):
        scan_pair(
            bests, query_ref, left_ref, lines_ref[0:1, :], lines_ref[1:2, :], codes_ref, core, part, left
        )
    sources = out_ref.shape[0]
    out_ref[...] = grouped(best_ref[...], sources, 0) + grouped(cross_ref[...], sources, 2 * GROUP)


def unpack_kernel(where_ref, back_ref, near_ref, far_ref, near_side_ref, far_side_ref, out_ref):
    half = near_ref.shape[0]
    rows = back_ref.shape[1]
    width = 2 * GROUP
    hot = (iota((2 * half, rows), 0) == back_ref[0:1, :]).astype(jnp.bfloat16)
    results = jnp.maximum(
        jnp.concatenate([near_ref[:, :width], far_ref[:, :width]], axis=0),
        jnp.concatenate([near_side_ref[:, width : 2 * width], far_side_ref[:, width : 2 * width]], axis=0),
    )
    total = jnp.zeros((width, rows), jnp.float32)
    for piece in split3(results):
        total = total + dot(piece, hot, ((0,), (0,)))
    mine = iota((width, rows), 0) == back_ref[1:2, :]
    out_ref[...] = jnp.sum(jnp.where(mine, total, 0.0), axis=0, keepdims=True)


AXES = ("dp", "help")
NY, NZ, NX = 4, 8, 4


def device(y, z, core, x):
    return ((y % NY * NZ + z % NZ) * 2 + core) * NX + x % NX


EVERY = [(y, z, c, x) for y in range(NY) for z in range(NZ) for c in range(2) for x in range(NX)]
SWAP = [(device(y, z, c, x), device(y, z, 1 - c, x)) for y, z, c, x in EVERY]
GROUPS = [[device(y, z, 0, x) for y in range(NY) for z in range(NZ)] for x in range(NX)] + [
    [device(y, z, 1, x) for z in range(NZ) for x in range(NX)] for y in range(NY)
]


def aside(step):
    return [
        (device(y, z, c, x), device(y, z, c, x + step) if c == 0 else device(y + step, z, c, x))
        for y, z, c, x in EVERY
    ]


ACROSS = [
    (device(y, z, c, x), device(y, z, 1, x + 1) if c == 0 else device(y + 1, z, 0, x))
    for y, z, c, x in EVERY
]


def exchange(array):
    return lax.all_to_all(
        array, AXES, split_axis=0, concat_axis=0, axis_index_groups=GROUPS, tiled=True
    )


def shards(embeddings, clusters, send_order):
    rows, depth = embeddings.shape
    half = lax.axis_size("dp") // 2
    data = GROUP * (depth // LANES)
    dp, x = lax.axis_index("dp"), lax.axis_index("help")
    core, y = dp % 2, dp // (2 * NZ)
    where = jnp.stack([jnp.where(core == 0, x, y), core, jnp.int32(NX)])
    half_float, full_float, whole = jnp.bfloat16, jnp.float32, jnp.int32
    send, notes, unit, back = call(
        send_kernel,
        "send",
        (where, embeddings, clusters.reshape(1, rows)),
        (
            ((half, data + NOTE, LANES), half_float),
            ((half, NOTE, LANES), half_float),
            ((rows, depth), half_float),
            ((8, rows), whole),
        ),
    )
    got = lax.ppermute(send, AXES, SWAP)
    (keep,) = call(
        keep_kernel, "keep", (where, unit, back), (((half, data, LANES), half_float),), flops=10**9
    )
    outgoing = jnp.concatenate([keep, got[:, :data], notes + got[:, data:]], axis=1)
    own = exchange(outgoing)
    left, right = lax.ppermute(own, AXES, aside(1)), lax.ppermute(own, AXES, aside(-1))
    row, lines = ((1, rows), full_float), ((8, rows), full_float)
    codes, groups = ((rows, LANES), full_float), ((half, LANES), full_float)
    best, own_rows, back = call(
        alone_kernel, "alone", (where, own, back), (row, lines, ((8, rows), whole)), (codes,), 10**9
    )
    best, right_rows, orders = call(
        right_kernel, "right", (where, best, own, right, own_rows), (row, lines, codes), (codes,), 10**9
    )
    (found,) = call(
        left_kernel,
        "left",
        (where, best, own, left, right, own_rows, right_rows, orders),
        (groups,),
        (row, row, codes),
        10**9,
    )
    near = exchange(found.reshape(half, 1, LANES)).reshape(half, LANES)
    sides = [lax.ppermute(near, AXES, pairs) for pairs in (SWAP, aside(1), ACROSS)]
    (out,) = call(unpack_kernel, "unpack", (where, back, near, *sides), (row,))
    return out.reshape(rows)


def solution(mesh):
    return jax.shard_map(
        shards,
        mesh=mesh,
        in_specs=(P(("dp", "help"), None), P(("dp", "help")), P(("dp", "help"))),
        out_specs=P(("dp", "help")),
        check_vma=False,
    )
```

```python
import jax
import jax.numpy as jnp
from jax import lax
from jax.experimental import pallas as pl
from jax.experimental.pallas import tpu as pltpu
from jax.sharding import PartitionSpec as P

LANES = 128
TILE = 256


def split3(x):
    high = x.astype(jnp.bfloat16)
    rest = x - high.astype(jnp.float32)
    mid = rest.astype(jnp.bfloat16)
    low = (rest - mid.astype(jnp.float32)).astype(jnp.bfloat16)
    return high, mid, low


def iota(shape, dim):
    return lax.broadcasted_iota(jnp.int32, shape, dim)


def dot(a, b, dims):
    return lax.dot_general(a, b, (dims, ((), ())), preferred_element_type=jnp.float32)


BITS = 4096.0
GROUP = 16
NOTE = 8


STEPS = (0, 1, 7, 2, 6, 3, 5, 4)
CUT = 5


def slot_of(clusters, where_ref, half):
    core, deep = where_ref[1], where_ref[4]
    owner = clusters // 2
    kind, index = owner // half, owner % half
    away = jnp.where(kind == core, 0, 1)
    by_row = kind == 0
    side = jnp.where(by_row, index // 8, index % 4) - jnp.where(by_row, where_ref[5], where_ref[6])
    ahead = jnp.where(by_row, index % 8, index // 4) - deep
    return index + away * half, (ahead & 7) * 4 + (side & 3) + away * half, away


def smem():
    return pl.BlockSpec(memory_space=pltpu.SMEM)


def vmem():
    return pl.BlockSpec(memory_space=pltpu.VMEM)


def call(kernel, name, ins, outs, scratch=(), flops=0):
    return pl.pallas_call(
        kernel,
        out_shape=tuple(jax.ShapeDtypeStruct(shape, kind) for shape, kind in outs),
        in_specs=[smem()] + [vmem()] * (len(ins) - 1),
        out_specs=(vmem(),) * len(outs),
        scratch_shapes=[pltpu.VMEM(shape, kind) for shape, kind in scratch],
        compiler_params=pltpu.CompilerParams(vmem_limit_bytes=48 * 2**20),
        cost_estimate=pl.CostEstimate(flops=flops, bytes_accessed=2**20, transcendentals=0),
        name=name,
    )(*ins)


def put_rows(out_ref, unit_ref, place, base):
    rows = unit_ref.shape[0]
    each = TILE // GROUP
    for start in range(0, rows // 2, TILE):
        pick = (iota((TILE, rows), 0) + (base + start) == place).astype(jnp.bfloat16)
        block = dot(pick, unit_ref[...], ((1,), (0,))).astype(jnp.bfloat16)
        first = start // GROUP
        for lane in range(block.shape[1] // LANES):
            out_ref[first : first + each, lane * GROUP : (lane + 1) * GROUP, :] = block[
                :, lane * LANES : (lane + 1) * LANES
            ].reshape(each, GROUP, LANES)


def send_kernel(where_ref, emb_ref, clu_ref, send_ref, notes_ref, unit_ref, rows_ref):
    rows = emb_ref.shape[0]
    half = send_ref.shape[0]
    clusters = clu_ref[...]
    home, slot, away = slot_of(clusters, where_ref, half)
    hot = (iota((2 * half, rows), 0) == slot).astype(jnp.bfloat16)
    before = (iota((rows, rows), 0) < iota((rows, rows), 1)).astype(jnp.bfloat16)
    count = dot(hot, before, ((1,), (0,)))
    rank = jnp.sum(hot.astype(jnp.float32) * count, axis=0, keepdims=True).astype(jnp.int32)
    spot = rank + away * GROUP
    place = slot * GROUP + rank
    rows_ref[...] = jnp.concatenate([home, spot, place, place] * 2, axis=0)
    bit = (clusters % 2).astype(jnp.float32)
    spots = jnp.where(iota((LANES, rows), 0) == spot, bit, 0.0).astype(jnp.bfloat16)
    labels = dot(hot, spots, ((1,), (1,))).astype(jnp.bfloat16)
    notes_ref[...] = jnp.broadcast_to(labels[:half, None, :], (half, NOTE, LANES))
    values = emb_ref[...].astype(jnp.float32)
    scale = lax.rsqrt(jnp.sum(values * values, axis=1, keepdims=True) + 1e-06)
    unit_ref[...] = (values * scale).astype(jnp.bfloat16)
    put_rows(send_ref, unit_ref, place, rows // 2)
    data = send_ref.shape[1] - NOTE
    send_ref[:, data:, :] = jnp.broadcast_to(labels[half:, None, :], (half, NOTE, LANES))


def keep_kernel(where_ref, unit_ref, rows_ref, keep_ref):
    put_rows(keep_ref, unit_ref, rows_ref[2:3, :], 0)


def cell_of(place, spot):
    turn = place // TILE - spot[0]
    return (turn & 3) * 8 + place % (TILE // 2) // GROUP


def origin_of(place, spot):
    k = place % (TILE // 2) // GROUP
    step = jnp.where(k % 2 == 1, (k + 1) // 2, 8 - k // 2)
    return place // TILE, (spot[1] - step) & 7


def source_of(place, spot, core):
    side, deep = origin_of(place, spot)
    return jnp.where(core == 0, side * 8 + deep, deep * 4 + side)


def lane_of(place):
    return place // (TILE // 2) % 2 * GROUP + place % GROUP


def order_of(place, spot, core, part):
    side, deep = origin_of(place, spot)
    flip, rank = place // (TILE // 2) % 2, place % GROUP
    from_core = jnp.where(flip == 0, core, 1 - core)
    y, x = jnp.where(core == 0, side, part), jnp.where(core == 0, part, side)
    return (((y * 8 + deep) * 2 + from_core) * 4 + x) * GROUP + rank


def tile_of(ref, index, spot):
    each = TILE // (2 * GROUP)
    data = (ref.shape[1] - NOTE) // 2
    here = pl.ds(((index - spot[0]) & 3) * each, each)
    lanes = []
    for base in range(0, data, GROUP):
        parts = [
            ref[here, start : start + GROUP, :].reshape(TILE // 2, LANES)
            for start in (base, data + base)
        ]
        lanes.append(jnp.concatenate(parts, axis=0))
    return jnp.concatenate(lanes, axis=1)


def notes_of(ref):
    data = ref.shape[1] - NOTE
    return (jnp.sum(ref[:, data:, :].astype(jnp.float32), axis=1) * (1.0 / NOTE)).astype(jnp.bfloat16)


def row_codes(lab, rows, spot, core, part):
    sources = lab.shape[0]
    width = 2 * GROUP
    place = iota((1, rows), 1)
    hot = (iota((sources, rows), 0) == cell_of(place, spot)).astype(jnp.bfloat16)
    spread = dot(lab[:, :width], hot, ((0,), (0,)))
    chosen = iota((width, rows), 0) == lane_of(place)
    label = jnp.sum(jnp.where(chosen, spread, 0.0), axis=0, keepdims=True)
    return label * BITS, label * BITS + order_of(place, spot, core, part).astype(jnp.float32)


def column_orders(rows, spot, core, part):
    place = iota((rows, LANES), 0)
    return order_of(place, spot, core, part).astype(jnp.float32)


def column_codes(lab, orders, spot):
    rows = orders.shape[0]
    sources = lab.shape[0]
    place = iota((rows, 1), 0)
    hot = (iota((rows, sources), 1) == cell_of(place, spot)).astype(jnp.bfloat16)
    spread = dot(hot, lab, ((1,), (0,)))
    chosen = iota((rows, LANES), 1) == lane_of(place)
    kept = jnp.where(chosen, spread, 0.0).astype(jnp.bfloat16)
    label = dot(kept, jnp.ones((LANES, LANES), jnp.bfloat16), ((1,), (0,)))
    return label * BITS + orders


def scan(best_ref, query_ref, key_ref, floor, ceiling, codes_ref, spot, pick):
    tiles = best_ref.shape[1] // TILE
    for query in range(tiles):
        queries = tile_of(query_ref, query, spot)
        here = slice(query * TILE, (query + 1) * TILE)
        best = best_ref[:, here]
        for key in range(tiles):
            if not pick(key, query):
                continue
            sims = dot(tile_of(key_ref, key, spot), queries, ((1,), (1,)))
            codes = codes_ref[key * TILE : (key + 1) * TILE, :]
            codes = jnp.concatenate([codes] * (TILE // LANES), axis=1)
            mask = (codes >= floor[:, here]) & (codes < ceiling[:, here])
            found = jnp.max(jnp.where(mask, sims, -1.0), axis=0, keepdims=True)
            best = jnp.maximum(best, found)
        best_ref[:, here] = best


def scan_pair(best_ref, query_ref, key_ref, floor, ceiling, codes_ref, spot, core, part, key_part):
    args = (best_ref, query_ref, key_ref, floor, ceiling, codes_ref, spot)

    @pl.when((core == 0) | (key_part < part))
    def _():
        scan(*args, lambda key, query: key <= query)

    @pl.when((core != 0) & (key_part < part))
    def _():
        scan(*args, lambda key, query: key > query)


def grouped(best, sources, spot, core, shift):
    rows = best.shape[1]
    mine = iota((sources, rows), 0) == source_of(iota((1, rows), 1), spot, core)
    spots = iota((rows, LANES), 1) == lane_of(iota((rows, 1), 0)) + shift
    pieces = [jnp.where(mine, piece.astype(jnp.float32), 0.0) for piece in split3(best)]
    spread = jnp.concatenate(pieces, axis=0).astype(jnp.bfloat16)
    total = dot(spread, spots.astype(jnp.bfloat16), ((1,), (0,)))
    return total[:sources] + total[sources : 2 * sources] + total[2 * sources :]


def parts_of(where_ref):
    me, core, parts = where_ref[0], where_ref[1], where_ref[2]
    spot = where_ref[3], where_ref[4]
    return spot, core, me, lax.rem(me + parts - 1, parts), lax.rem(me + 1, parts)


def alone_kernel(where_ref, own_ref, back_ref, best_ref, rows_ref, kept_ref, codes_ref):
    rows = best_ref.shape[1]
    spot, core, me, _, _ = parts_of(where_ref)
    kept_ref[...] = back_ref[...]
    lab = notes_of(own_ref)
    floor, ceiling = row_codes(lab, rows, spot, core, me)
    rows_ref[...] = jnp.concatenate([floor, ceiling] * 4, axis=0)
    codes_ref[...] = column_codes(lab, column_orders(rows, spot, core, me), spot)
    best_ref[...] = jnp.full((1, rows), -1.0, jnp.float32)
    args = (best_ref, own_ref, own_ref, floor, ceiling, codes_ref, spot)
    scan(*args, lambda key, query: key <= query)

    @pl.when(core != 0)
    def _():
        scan(*args, lambda key, query: key > query)


def right_kernel(
    where_ref, alone_ref, own_ref, right_ref, rows_ref, best_ref, right_rows_ref, orders_ref, codes_ref
):
    rows = best_ref.shape[1]
    spot, core, me, left, right = parts_of(where_ref)
    best_ref[...] = alone_ref[...]
    lab = notes_of(right_ref)
    floor, ceiling = row_codes(lab, rows, spot, core, right)
    right_rows_ref[...] = jnp.concatenate([floor, ceiling] * 4, axis=0)
    orders_ref[...] = column_orders(rows, spot, core, left)
    codes_ref[...] = column_codes(lab, column_orders(rows, spot, core, right), spot)
    scan_pair(
        best_ref, own_ref, right_ref, rows_ref[0:1, :], rows_ref[1:2, :], codes_ref, spot, core, me, right
    )


def left_kernel(
    where_ref, found_ref, own_ref, left_ref, right_ref, rows_ref, right_rows_ref, orders_ref,
    out_ref, best_ref, cross_ref, codes_ref,
):
    rows = best_ref.shape[1]
    spot, core, me, left, right = parts_of(where_ref)
    best_ref[...] = found_ref[...]
    cross_ref[...] = jnp.full((1, rows), -1.0, jnp.float32)
    codes_ref[...] = column_codes(notes_of(left_ref), orders_ref[...], spot)
    for bests, query_ref, lines_ref, part in (
        (best_ref, own_ref, rows_ref, me),
        (cross_ref, right_ref, right_rows_ref, right),
    ):
        scan_pair(
            bests, query_ref, left_ref, lines_ref[0:1, :], lines_ref[1:2, :], codes_ref, spot, core, part, left
        )
    sources = out_ref.shape[0]
    out_ref[...] = grouped(
        best_ref[...], sources, spot, core, 0
    ) + grouped(cross_ref[...], sources, spot, core, 2 * GROUP)


def unpack_kernel(where_ref, back_ref, near_ref, far_ref, near_side_ref, far_side_ref, out_ref):
    half = near_ref.shape[0]
    rows = back_ref.shape[1]
    width = 2 * GROUP
    hot = (iota((2 * half, rows), 0) == back_ref[0:1, :]).astype(jnp.bfloat16)
    results = jnp.maximum(
        jnp.concatenate([near_ref[:, :width], far_ref[:, :width]], axis=0),
        jnp.concatenate([near_side_ref[:, width : 2 * width], far_side_ref[:, width : 2 * width]], axis=0),
    )
    total = jnp.zeros((width, rows), jnp.float32)
    for piece in split3(results):
        total = total + dot(piece, hot, ((0,), (0,)))
    mine = iota((width, rows), 0) == back_ref[1:2, :]
    out_ref[...] = jnp.sum(jnp.where(mine, total, 0.0), axis=0, keepdims=True)


AXES = ("dp", "help")
NY, NZ, NX = 4, 8, 4


def device(y, z, core, x):
    return ((y % NY * NZ + z % NZ) * 2 + core) * NX + x % NX


EVERY = [(y, z, c, x) for y in range(NY) for z in range(NZ) for c in range(2) for x in range(NX)]
SWAP = [(device(y, z, c, x), device(y, z, 1 - c, x)) for y, z, c, x in EVERY]
GROUPS = [[device(y, z, 0, x) for y in range(NY) for z in range(NZ)] for x in range(NX)] + [
    [device(y, z, 1, x) for z in range(NZ) for x in range(NX)] for y in range(NY)
]


def aside(step):
    return [
        (device(y, z, c, x), device(y, z, c, x + step) if c == 0 else device(y + step, z, c, x))
        for y, z, c, x in EVERY
    ]


ACROSS = [
    (device(y, z, c, x), device(y, z, 1, x + 1) if c == 0 else device(y + 1, z, 0, x))
    for y, z, c, x in EVERY
]


def ahead(step):
    return [(device(y, z, c, x), device(y, z + step, c, x)) for y, z, c, x in EVERY]


def sideways(step):
    return [
        (device(y, z, c, x), device(y + step, z, c, x) if c == 0 else device(y, z, c, x + step))
        for y, z, c, x in EVERY
    ]


def exchange(array):
    return lax.all_to_all(
        array, AXES, split_axis=0, concat_axis=0, axis_index_groups=GROUPS, tiled=True
    )


def merge(early, late):
    rest = NZ - CUT
    return jnp.concatenate(
        [
            cells[turn * size : (turn + 1) * size]
            for turn in range(NY)
            for cells, size in ((early, CUT), (late, rest))
        ],
        axis=0,
    )


def shards(embeddings, clusters, send_order):
    rows, depth = embeddings.shape
    half = lax.axis_size("dp") // 2
    data = GROUP * (depth // LANES)
    dp, x = lax.axis_index("dp"), lax.axis_index("help")
    core, y = dp % 2, dp // (2 * NZ)
    deep, first = dp // 2 % NZ, core == 0
    part, side = jnp.where(first, x, y), jnp.where(first, y, x)
    where = jnp.stack([part, core, jnp.int32(NX), side, deep, y, x])
    half_float, full_float, whole = jnp.bfloat16, jnp.float32, jnp.int32
    send, notes, unit, back = call(
        send_kernel,
        "send",
        (where, embeddings, clusters.reshape(1, rows)),
        (
            ((half, data + NOTE, LANES), half_float),
            ((half, NOTE, LANES), half_float),
            ((rows, depth), half_float),
            ((8, rows), whole),
        ),
    )
    got = lax.ppermute(send, AXES, SWAP)
    (keep,) = call(
        keep_kernel, "keep", (where, unit, back), (((half, data, LANES), half_float),), flops=10**9
    )
    outgoing = jnp.concatenate([keep, got[:, :data], notes + got[:, data:]], axis=1)
    passed = {
        step: outgoing[step * NY : (step + 1) * NY]
        if step == 0
        else lax.ppermute(outgoing[step * NY : (step + 1) * NY], AXES, ahead(step))
        for step in STEPS
    }
    halves = []
    for steps in (STEPS[:CUT], STEPS[CUT:]):
        turned = []
        for turn in (0, 3, 2, 1):
            cells = jnp.concatenate([passed[step][turn : turn + 1] for step in steps], axis=0)
            turned.append(lax.ppermute(cells, AXES, sideways(turn)) if turn else cells)
        halves.append(jnp.concatenate(turned, axis=0))
    own = merge(*halves)
    left = merge(*[lax.ppermute(cells, AXES, aside(1)) for cells in halves])
    right = merge(*[lax.ppermute(cells, AXES, aside(-1)) for cells in halves])
    row, lines = ((1, rows), full_float), ((8, rows), full_float)
    codes, groups = ((rows, LANES), full_float), ((half, LANES), full_float)
    best, own_rows, back = call(
        alone_kernel, "alone", (where, own, back), (row, lines, ((8, rows), whole)), (codes,), 10**9
    )
    best, right_rows, orders = call(
        right_kernel, "right", (where, best, own, right, own_rows), (row, lines, codes), (codes,), 10**9
    )
    (found,) = call(
        left_kernel,
        "left",
        (where, best, own, left, right, own_rows, right_rows, orders),
        (groups,),
        (row, row, codes),
        10**9,
    )
    near = exchange(found.reshape(half, 1, LANES)).reshape(half, LANES)
    sides = [lax.ppermute(near, AXES, pairs) for pairs in (SWAP, aside(1), ACROSS)]
    (out,) = call(unpack_kernel, "unpack", (where, back, near, *sides), (row,))
    return out.reshape(rows)


def solution(mesh):
    return jax.shard_map(
        shards,
        mesh=mesh,
        in_specs=(P(("dp", "help"), None), P(("dp", "help")), P(("dp", "help"))),
        out_specs=P(("dp", "help")),
        check_vma=False,
    )
```

```python
import jax
import jax.numpy as jnp
from jax import lax
from jax.experimental import pallas as pl
from jax.experimental.pallas import tpu as pltpu
from jax.sharding import PartitionSpec as P

LANES = 128
TILE = 256


def split3(x):
    high = x.astype(jnp.bfloat16)
    rest = x - high.astype(jnp.float32)
    mid = rest.astype(jnp.bfloat16)
    low = (rest - mid.astype(jnp.float32)).astype(jnp.bfloat16)
    return high, mid, low


def iota(shape, dim):
    return lax.broadcasted_iota(jnp.int32, shape, dim)


def dot(a, b, dims):
    return lax.dot_general(a, b, (dims, ((), ())), preferred_element_type=jnp.float32)


BITS = 4096.0
GROUP = 16
NOTE = 8


def slot_of(clusters, core, half):
    owner = clusters // 2
    away = jnp.where(owner // half == core, 0, 1)
    return owner % half + away * half, away


def smem():
    return pl.BlockSpec(memory_space=pltpu.SMEM)


def vmem():
    return pl.BlockSpec(memory_space=pltpu.VMEM)


def call(kernel, name, ins, outs, scratch=(), flops=0):
    return pl.pallas_call(
        kernel,
        out_shape=tuple(jax.ShapeDtypeStruct(shape, kind) for shape, kind in outs),
        in_specs=[smem()] + [vmem()] * (len(ins) - 1),
        out_specs=(vmem(),) * len(outs),
        scratch_shapes=[pltpu.VMEM(shape, kind) for shape, kind in scratch],
        compiler_params=pltpu.CompilerParams(vmem_limit_bytes=48 * 2**20),
        cost_estimate=pl.CostEstimate(flops=flops, bytes_accessed=2**20, transcendentals=0),
        name=name,
    )(*ins)


def put_rows(out_ref, unit_ref, place, base):
    rows = unit_ref.shape[0]
    each = TILE // GROUP
    for start in range(0, rows // 2, TILE):
        pick = (iota((TILE, rows), 0) + (base + start) == place).astype(jnp.bfloat16)
        block = dot(pick, unit_ref[...], ((1,), (0,))).astype(jnp.bfloat16)
        first = start // GROUP
        for lane in range(block.shape[1] // LANES):
            out_ref[first : first + each, lane * GROUP : (lane + 1) * GROUP, :] = block[
                :, lane * LANES : (lane + 1) * LANES
            ].reshape(each, GROUP, LANES)


def rank_kernel(where_ref, clu_ref, rows_ref, labels_ref):
    half = labels_ref.shape[0] // 2
    rows = clu_ref.shape[1]
    clusters = clu_ref[...]
    slot, away = slot_of(clusters, where_ref[1], half)
    hot = (iota((2 * half, rows), 0) == slot).astype(jnp.bfloat16)
    before = (iota((rows, rows), 0) < iota((rows, rows), 1)).astype(jnp.bfloat16)
    count = dot(hot, before, ((1,), (0,)))
    rank = jnp.sum(hot.astype(jnp.float32) * count, axis=0, keepdims=True).astype(jnp.int32)
    spot = rank + away * GROUP
    place = slot * GROUP + rank
    rows_ref[...] = jnp.concatenate([slot, spot, place, place] * 2, axis=0)
    bit = (clusters % 2).astype(jnp.float32)
    spots = jnp.where(iota((LANES, rows), 0) == spot, bit, 0.0).astype(jnp.bfloat16)
    labels_ref[...] = dot(hot, spots, ((1,), (1,))).astype(jnp.bfloat16)


def send_kernel(where_ref, emb_ref, rows_ref, labels_ref, send_ref, notes_ref, unit_ref):
    rows = emb_ref.shape[0]
    half = send_ref.shape[0]
    labels = labels_ref[...]
    notes_ref[...] = jnp.broadcast_to(labels[:half, None, :], (half, NOTE, LANES))
    values = emb_ref[...].astype(jnp.float32)
    scale = lax.rsqrt(jnp.sum(values * values, axis=1, keepdims=True) + 1e-06)
    unit_ref[...] = (values * scale).astype(jnp.bfloat16)
    put_rows(send_ref, unit_ref, rows_ref[2:3, :], rows // 2)
    data = send_ref.shape[1] - NOTE
    send_ref[:, data:, :] = jnp.broadcast_to(labels[half:, None, :], (half, NOTE, LANES))


def keep_kernel(where_ref, unit_ref, rows_ref, keep_ref):
    put_rows(keep_ref, unit_ref, rows_ref[2:3, :], 0)


def source_of(place):
    return place // TILE * (TILE // (2 * GROUP)) + place % (TILE // 2) // GROUP


def lane_of(place):
    return place // (TILE // 2) % 2 * GROUP + place % GROUP


def order_of(place, core, part):
    source, flip, rank = source_of(place), place // (TILE // 2) % 2, place % GROUP
    from_core = jnp.where(flip == 0, core, 1 - core)
    by_row = (source * 2 + from_core) * 4 + part
    by_column = ((part * 8 + source // 4) * 2 + from_core) * 4 + source % 4
    return jnp.where(core == 0, by_row, by_column) * GROUP + rank


def tile_of(ref, index):
    each = TILE // (2 * GROUP)
    data = (ref.shape[1] - NOTE) // 2
    here = slice(index * each, (index + 1) * each)
    lanes = []
    for base in range(0, data, GROUP):
        parts = [
            ref[here, start : start + GROUP, :].reshape(TILE // 2, LANES)
            for start in (base, data + base)
        ]
        lanes.append(jnp.concatenate(parts, axis=0))
    return jnp.concatenate(lanes, axis=1)


def notes_of(ref):
    data = ref.shape[1] - NOTE
    return (jnp.sum(ref[:, data:, :].astype(jnp.float32), axis=1) * (1.0 / NOTE)).astype(jnp.bfloat16)


def row_codes(lab, rows, core, part):
    sources = lab.shape[0]
    width = 2 * GROUP
    place = iota((1, rows), 1)
    hot = (iota((sources, rows), 0) == source_of(place)).astype(jnp.bfloat16)
    spread = dot(lab[:, :width], hot, ((0,), (0,)))
    chosen = iota((width, rows), 0) == lane_of(place)
    label = jnp.sum(jnp.where(chosen, spread, 0.0), axis=0, keepdims=True)
    return label * BITS, label * BITS + order_of(place, core, part).astype(jnp.float32)


def column_orders(rows, core, part):
    place = iota((rows, LANES), 0)
    return order_of(place, core, part).astype(jnp.float32)


def column_codes(lab, orders):
    rows = orders.shape[0]
    sources = lab.shape[0]
    place = iota((rows, 1), 0)
    hot = (iota((rows, sources), 1) == source_of(place)).astype(jnp.bfloat16)
    spread = dot(hot, lab, ((1,), (0,)))
    chosen = iota((rows, LANES), 1) == lane_of(place)
    kept = jnp.where(chosen, spread, 0.0).astype(jnp.bfloat16)
    label = dot(kept, jnp.ones((LANES, LANES), jnp.bfloat16), ((1,), (0,)))
    return label * BITS + orders


def scan(best_ref, query_ref, key_ref, floor, ceiling, codes_ref, pick):
    tiles = best_ref.shape[1] // TILE
    for query in range(tiles):
        queries = tile_of(query_ref, query)
        here = slice(query * TILE, (query + 1) * TILE)
        best = best_ref[:, here]
        for key in range(tiles):
            if not pick(key, query):
                continue
            sims = dot(tile_of(key_ref, key), queries, ((1,), (1,)))
            codes = codes_ref[key * TILE : (key + 1) * TILE, :]
            codes = jnp.concatenate([codes] * (TILE // LANES), axis=1)
            mask = (codes >= floor[:, here]) & (codes < ceiling[:, here])
            found = jnp.max(jnp.where(mask, sims, -1.0), axis=0, keepdims=True)
            best = jnp.maximum(best, found)
        best_ref[:, here] = best


def scan_pair(best_ref, query_ref, key_ref, floor, ceiling, codes_ref, core, part, key_part):
    args = (best_ref, query_ref, key_ref, floor, ceiling, codes_ref)

    @pl.when((core == 0) | (key_part < part))
    def _():
        scan(*args, lambda key, query: key <= query)

    @pl.when((core != 0) & (key_part < part))
    def _():
        scan(*args, lambda key, query: key > query)


def store_groups(out_ref, best):
    sources = out_ref.shape[0]
    rows = best.shape[1]
    mine = iota((sources, rows), 0) == source_of(iota((1, rows), 1))
    spots = (iota((rows, LANES), 1) == lane_of(iota((rows, 1), 0))).astype(jnp.bfloat16)
    pieces = [jnp.where(mine, piece.astype(jnp.float32), 0.0) for piece in split3(best)]
    total = dot(jnp.concatenate(pieces, axis=0).astype(jnp.bfloat16), spots, ((1,), (0,)))
    out_ref[...] = total[:sources] + total[sources : 2 * sources] + total[2 * sources :]


def parts_of(where_ref):
    me, core, parts = where_ref[0], where_ref[1], where_ref[2]
    return core, me, lax.rem(me + parts - 1, parts), lax.rem(me + 1, parts)


def alone_kernel(where_ref, own_ref, back_ref, best_ref, rows_ref, kept_ref, codes_ref):
    rows = best_ref.shape[1]
    core, me, _, _ = parts_of(where_ref)
    kept_ref[...] = back_ref[...]
    lab = notes_of(own_ref)
    floor, ceiling = row_codes(lab, rows, core, me)
    rows_ref[...] = jnp.concatenate([floor, ceiling] * 4, axis=0)
    codes_ref[...] = column_codes(lab, column_orders(rows, core, me))
    best_ref[...] = jnp.full((1, rows), -1.0, jnp.float32)
    scan(best_ref, own_ref, own_ref, floor, ceiling, codes_ref, lambda key, query: key <= query)


def right_kernel(
    where_ref, alone_ref, own_ref, right_ref, rows_ref, best_ref, right_rows_ref, orders_ref, codes_ref
):
    rows = best_ref.shape[1]
    core, me, left, right = parts_of(where_ref)
    best_ref[...] = alone_ref[...]
    lab = notes_of(right_ref)
    floor, ceiling = row_codes(lab, rows, core, right)
    right_rows_ref[...] = jnp.concatenate([floor, ceiling] * 4, axis=0)
    orders_ref[...] = column_orders(rows, core, left)
    codes_ref[...] = column_codes(lab, column_orders(rows, core, right))
    scan_pair(
        best_ref, own_ref, right_ref, rows_ref[0:1, :], rows_ref[1:2, :], codes_ref, core, me, right
    )


def cross_kernel(where_ref, left_ref, right_ref, rows_ref, orders_ref, out_ref, codes_ref, best_ref):
    rows = best_ref.shape[1]
    core, _, left, right = parts_of(where_ref)
    codes_ref[...] = column_codes(notes_of(left_ref), orders_ref[...])
    best_ref[...] = jnp.full((1, rows), -1.0, jnp.float32)
    scan_pair(
        best_ref, right_ref, left_ref, rows_ref[0:1, :], rows_ref[1:2, :], codes_ref, core, right, left
    )
    store_groups(out_ref, best_ref[...])


def left_kernel(where_ref, found_ref, own_ref, left_ref, rows_ref, codes_ref, out_ref, best_ref):
    core, me, left, _ = parts_of(where_ref)
    best_ref[...] = found_ref[...]
    scan_pair(
        best_ref, own_ref, left_ref, rows_ref[0:1, :], rows_ref[1:2, :], codes_ref, core, me, left
    )
    store_groups(out_ref, best_ref[...])


def unpack_kernel(where_ref, back_ref, near_ref, far_ref, out_ref):
    half = near_ref.shape[0]
    rows = back_ref.shape[1]
    width = 2 * GROUP
    hot = (iota((2 * half, rows), 0) == back_ref[0:1, :]).astype(jnp.bfloat16)
    results = jnp.concatenate([near_ref[:, :width], far_ref[:, :width]], axis=0)
    total = jnp.zeros((width, rows), jnp.float32)
    for piece in split3(results):
        total = total + dot(piece, hot, ((0,), (0,)))
    mine = iota((width, rows), 0) == back_ref[1:2, :]
    out_ref[...] = jnp.sum(jnp.where(mine, total, 0.0), axis=0, keepdims=True)


AXES = ("dp", "help")
NY, NZ, NX = 4, 8, 4


def device(y, z, core, x):
    return ((y % NY * NZ + z % NZ) * 2 + core) * NX + x % NX


EVERY = [(y, z, c, x) for y in range(NY) for z in range(NZ) for c in range(2) for x in range(NX)]
SWAP = [(device(y, z, c, x), device(y, z, 1 - c, x)) for y, z, c, x in EVERY]
GROUPS = [[device(y, z, 0, x) for y in range(NY) for z in range(NZ)] for x in range(NX)] + [
    [device(y, z, 1, x) for z in range(NZ) for x in range(NX)] for y in range(NY)
]


def aside(step):
    return [
        (device(y, z, c, x), device(y, z, c, x + step) if c == 0 else device(y + step, z, c, x))
        for y, z, c, x in EVERY
    ]


def exchange(array):
    return lax.all_to_all(
        array, AXES, split_axis=0, concat_axis=0, axis_index_groups=GROUPS, tiled=True
    )


def shards(embeddings, clusters, send_order):
    rows, depth = embeddings.shape
    half = lax.axis_size("dp") // 2
    data = GROUP * (depth // LANES)
    dp, x = lax.axis_index("dp"), lax.axis_index("help")
    core, y = dp % 2, dp // (2 * NZ)
    where = jnp.stack([jnp.where(core == 0, x, y), core, jnp.int32(NX)])
    half_float, full_float, whole = jnp.bfloat16, jnp.float32, jnp.int32
    back, labels = call(
        rank_kernel,
        "rank",
        (where, clusters.reshape(1, rows)),
        (((8, rows), whole), ((2 * half, LANES), half_float)),
        flops=10**9,
    )
    send, notes, unit = call(
        send_kernel,
        "send",
        (where, embeddings, back, labels),
        (
            ((half, data + NOTE, LANES), half_float),
            ((half, NOTE, LANES), half_float),
            ((rows, depth), half_float),
        ),
        flops=10**9,
    )
    got = lax.ppermute(send, AXES, SWAP)
    (keep,) = call(
        keep_kernel, "keep", (where, unit, back), (((half, data, LANES), half_float),), flops=10**9
    )
    outgoing = jnp.concatenate([keep, got[:, :data], notes + got[:, data:]], axis=1)
    own = exchange(outgoing)
    left, right = lax.ppermute(own, AXES, aside(1)), lax.ppermute(own, AXES, aside(-1))
    row, lines = ((1, rows), full_float), ((8, rows), full_float)
    codes, groups = ((rows, LANES), full_float), ((half, LANES), full_float)
    best, own_rows, back = call(
        alone_kernel, "alone", (where, own, back), (row, lines, ((8, rows), whole)), (codes,), 10**9
    )
    best, right_rows, orders = call(
        right_kernel, "right", (where, best, own, right, own_rows), (row, lines, codes), (codes,), 10**9
    )
    cross, left_codes = call(
        cross_kernel, "cross", (where, left, right, right_rows, orders), (groups, codes), (row,), 10**9
    )
    cross = lax.ppermute(cross, AXES, aside(1))
    (best,) = call(
        left_kernel, "left", (where, best, own, left, own_rows, left_codes), (groups,), (row,), 10**9
    )
    best = jnp.maximum(best, cross)
    near = exchange(best.reshape(half, 1, LANES)).reshape(half, LANES)
    far = lax.ppermute(near, AXES, SWAP)
    (out,) = call(unpack_kernel, "unpack", (where, back, near, far), (row,))
    return out.reshape(rows)


def solution(mesh):
    return jax.shard_map(
        shards,
        mesh=mesh,
        in_specs=(P(("dp", "help"), None), P(("dp", "help")), P(("dp", "help"))),
        out_specs=P(("dp", "help")),
        check_vma=False,
    )
```

```python
import jax
import jax.numpy as jnp
from jax import lax
from jax.experimental import pallas as pl
from jax.experimental.pallas import tpu as pltpu
from jax.sharding import PartitionSpec as P

LANES = 128
TILE = 256


def split3(x):
    high = x.astype(jnp.bfloat16)
    rest = x - high.astype(jnp.float32)
    mid = rest.astype(jnp.bfloat16)
    low = (rest - mid.astype(jnp.float32)).astype(jnp.bfloat16)
    return high, mid, low


def iota(shape, dim):
    return lax.broadcasted_iota(jnp.int32, shape, dim)


def dot(a, b, dims):
    return lax.dot_general(a, b, (dims, ((), ())), preferred_element_type=jnp.float32)


BITS = 4096.0
GROUP = 16
NOTE = 8


def slot_of(clusters, core, half):
    owner = clusters // 2
    away = jnp.where(owner // half == core, 0, 1)
    return owner % half + away * half, away


def smem():
    return pl.BlockSpec(memory_space=pltpu.SMEM)


def vmem():
    return pl.BlockSpec(memory_space=pltpu.VMEM)


def call(kernel, name, ins, outs, scratch=(), flops=0):
    return pl.pallas_call(
        kernel,
        out_shape=tuple(jax.ShapeDtypeStruct(shape, kind) for shape, kind in outs),
        in_specs=[smem()] + [vmem()] * (len(ins) - 1),
        out_specs=(vmem(),) * len(outs),
        scratch_shapes=[pltpu.VMEM(shape, kind) for shape, kind in scratch],
        compiler_params=pltpu.CompilerParams(vmem_limit_bytes=48 * 2**20),
        cost_estimate=pl.CostEstimate(flops=flops, bytes_accessed=2**20, transcendentals=0),
        name=name,
    )(*ins)


def put_rows(out_ref, unit_ref, place, base):
    rows = unit_ref.shape[0]
    each = TILE // GROUP
    for start in range(0, rows // 2, TILE):
        pick = (iota((TILE, rows), 0) + (base + start) == place).astype(jnp.bfloat16)
        block = dot(pick, unit_ref[...], ((1,), (0,))).astype(jnp.bfloat16)
        first = start // GROUP
        for lane in range(block.shape[1] // LANES):
            out_ref[first : first + each, lane * GROUP : (lane + 1) * GROUP, :] = block[
                :, lane * LANES : (lane + 1) * LANES
            ].reshape(each, GROUP, LANES)


def rank_kernel(where_ref, clu_ref, rows_ref, labels_ref):
    half = labels_ref.shape[0] // 2
    rows = clu_ref.shape[1]
    clusters = clu_ref[...]
    slot, away = slot_of(clusters, where_ref[1], half)
    hot = (iota((2 * half, rows), 0) == slot).astype(jnp.bfloat16)
    before = (iota((rows, rows), 0) < iota((rows, rows), 1)).astype(jnp.bfloat16)
    count = dot(hot, before, ((1,), (0,)))
    rank = jnp.sum(hot.astype(jnp.float32) * count, axis=0, keepdims=True).astype(jnp.int32)
    spot = rank + away * GROUP
    place = slot * GROUP + rank
    rows_ref[...] = jnp.concatenate([slot, spot, place, place] * 2, axis=0)
    bit = (clusters % 2).astype(jnp.float32)
    spots = jnp.where(iota((LANES, rows), 0) == spot, bit, 0.0).astype(jnp.bfloat16)
    labels_ref[...] = dot(hot, spots, ((1,), (1,))).astype(jnp.bfloat16)


def send_kernel(where_ref, emb_ref, rows_ref, labels_ref, send_ref, notes_ref, unit_ref):
    rows = emb_ref.shape[0]
    half = send_ref.shape[0]
    labels = labels_ref[...]
    notes_ref[...] = jnp.broadcast_to(labels[:half, None, :], (half, NOTE, LANES))
    values = emb_ref[...].astype(jnp.float32)
    scale = lax.rsqrt(jnp.sum(values * values, axis=1, keepdims=True) + 1e-06)
    unit_ref[...] = (values * scale).astype(jnp.bfloat16)
    put_rows(send_ref, unit_ref, rows_ref[2:3, :], rows // 2)
    data = send_ref.shape[1] - NOTE
    send_ref[:, data:, :] = jnp.broadcast_to(labels[half:, None, :], (half, NOTE, LANES))


def keep_kernel(where_ref, unit_ref, rows_ref, keep_ref):
    put_rows(keep_ref, unit_ref, rows_ref[2:3, :], 0)


def source_of(place):
    return place // TILE * (TILE // (2 * GROUP)) + place % (TILE // 2) // GROUP


def lane_of(place):
    return place // (TILE // 2) % 2 * GROUP + place % GROUP


def order_of(place, core, part):
    source, flip, rank = source_of(place), place // (TILE // 2) % 2, place % GROUP
    from_core = jnp.where(flip == 0, core, 1 - core)
    by_row = (source * 2 + from_core) * 4 + part
    by_column = ((part * 8 + source // 4) * 2 + from_core) * 4 + source % 4
    return jnp.where(core == 0, by_row, by_column) * GROUP + rank


def tile_of(ref, index):
    each = TILE // (2 * GROUP)
    data = (ref.shape[1] - NOTE) // 2
    here = slice(index * each, (index + 1) * each)
    lanes = []
    for base in range(0, data, GROUP):
        parts = [
            ref[here, start : start + GROUP, :].reshape(TILE // 2, LANES)
            for start in (base, data + base)
        ]
        lanes.append(jnp.concatenate(parts, axis=0))
    return jnp.concatenate(lanes, axis=1)


def notes_of(ref):
    data = ref.shape[1] - NOTE
    return (jnp.sum(ref[:, data:, :].astype(jnp.float32), axis=1) * (1.0 / NOTE)).astype(jnp.bfloat16)


def row_codes(lab, rows, core, part):
    sources = lab.shape[0]
    width = 2 * GROUP
    place = iota((1, rows), 1)
    hot = (iota((sources, rows), 0) == source_of(place)).astype(jnp.bfloat16)
    spread = dot(lab[:, :width], hot, ((0,), (0,)))
    chosen = iota((width, rows), 0) == lane_of(place)
    label = jnp.sum(jnp.where(chosen, spread, 0.0), axis=0, keepdims=True)
    return label * BITS, label * BITS + order_of(place, core, part).astype(jnp.float32)


def column_orders(rows, core, part):
    place = iota((rows, LANES), 0)
    return order_of(place, core, part).astype(jnp.float32)


def spots_of(rows):
    return (iota((rows, LANES), 1) == lane_of(iota((rows, 1), 0))).astype(jnp.bfloat16)


def cells_of(rows, sources):
    return (iota((rows, sources), 1) == source_of(iota((rows, 1), 0))).astype(jnp.bfloat16)


def mine_of(sources, rows):
    return (iota((sources, rows), 0) == source_of(iota((1, rows), 1))).astype(jnp.bfloat16)


def column_codes(lab, orders, cells, spots):
    kept = dot(cells, lab, ((1,), (0,))).astype(jnp.bfloat16) * spots
    label = dot(kept, jnp.ones((LANES, LANES), jnp.bfloat16), ((1,), (0,)))
    return label * BITS + orders


def scan(best_ref, query_ref, key_ref, floor, ceiling, codes_ref, pick):
    tiles = best_ref.shape[1] // TILE
    for query in range(tiles):
        queries = tile_of(query_ref, query)
        here = slice(query * TILE, (query + 1) * TILE)
        best = best_ref[:, here]
        for key in range(tiles):
            if not pick(key, query):
                continue
            sims = dot(tile_of(key_ref, key), queries, ((1,), (1,)))
            codes = codes_ref[key * TILE : (key + 1) * TILE, :]
            codes = jnp.concatenate([codes] * (TILE // LANES), axis=1)
            mask = (codes >= floor[:, here]) & (codes < ceiling[:, here])
            found = jnp.max(jnp.where(mask, sims, -1.0), axis=0, keepdims=True)
            best = jnp.maximum(best, found)
        best_ref[:, here] = best


def scan_pair(best_ref, query_ref, key_ref, floor, ceiling, codes_ref, core, part, key_part):
    args = (best_ref, query_ref, key_ref, floor, ceiling, codes_ref)

    @pl.when((core == 0) | (key_part < part))
    def _():
        scan(*args, lambda key, query: key <= query)

    @pl.when((core != 0) & (key_part < part))
    def _():
        scan(*args, lambda key, query: key > query)


def store_groups(out_ref, best, mine, spots):
    sources = out_ref.shape[0]
    spread = jnp.concatenate([mine * piece for piece in split3(best)], axis=0)
    total = dot(spread, spots, ((1,), (0,)))
    out_ref[...] = total[:sources] + total[sources : 2 * sources] + total[2 * sources :]


def parts_of(where_ref):
    me, core, parts = where_ref[0], where_ref[1], where_ref[2]
    return core, me, lax.rem(me + parts - 1, parts), lax.rem(me + 1, parts)


def alone_kernel(
    where_ref, own_ref, back_ref, best_ref, rows_ref, kept_ref, spots_ref, cells_ref, mine_ref,
    left_orders_ref, right_orders_ref, codes_ref,
):
    rows = best_ref.shape[1]
    sources = own_ref.shape[0]
    spots_ref[...] = spots_of(rows)
    cells_ref[...] = cells_of(rows, sources)
    mine_ref[...] = mine_of(sources, rows)
    core, me, left, right = parts_of(where_ref)
    left_orders_ref[...] = column_orders(rows, core, left)
    right_orders_ref[...] = column_orders(rows, core, right)
    kept_ref[...] = back_ref[...]
    lab = notes_of(own_ref)
    floor, ceiling = row_codes(lab, rows, core, me)
    rows_ref[...] = jnp.concatenate([floor, ceiling] * 4, axis=0)
    codes_ref[...] = column_codes(lab, column_orders(rows, core, me), cells_ref[...], spots_ref[...])
    best_ref[...] = jnp.full((1, rows), -1.0, jnp.float32)
    scan(best_ref, own_ref, own_ref, floor, ceiling, codes_ref, lambda key, query: key <= query)


def right_kernel(
    where_ref, alone_ref, own_ref, right_ref, rows_ref, orders_ref, spots_ref, cells_ref,
    best_ref, right_rows_ref, codes_ref,
):
    rows = best_ref.shape[1]
    core, me, _, right = parts_of(where_ref)
    best_ref[...] = alone_ref[...]
    lab = notes_of(right_ref)
    floor, ceiling = row_codes(lab, rows, core, right)
    right_rows_ref[...] = jnp.concatenate([floor, ceiling] * 4, axis=0)
    codes_ref[...] = column_codes(lab, orders_ref[...], cells_ref[...], spots_ref[...])
    scan_pair(
        best_ref, own_ref, right_ref, rows_ref[0:1, :], rows_ref[1:2, :], codes_ref, core, me, right
    )


def cross_kernel(
    where_ref, left_ref, right_ref, rows_ref, orders_ref, spots_ref, cells_ref, mine_ref,
    out_ref, codes_ref, best_ref,
):
    rows = best_ref.shape[1]
    core, _, left, right = parts_of(where_ref)
    codes_ref[...] = column_codes(notes_of(left_ref), orders_ref[...], cells_ref[...], spots_ref[...])
    best_ref[...] = jnp.full((1, rows), -1.0, jnp.float32)
    scan_pair(
        best_ref, right_ref, left_ref, rows_ref[0:1, :], rows_ref[1:2, :], codes_ref, core, right, left
    )
    store_groups(out_ref, best_ref[...], mine_ref[...], spots_ref[...])


def left_kernel(
    where_ref, found_ref, own_ref, left_ref, rows_ref, codes_ref, spots_ref, mine_ref, out_ref, best_ref
):
    core, me, left, _ = parts_of(where_ref)
    best_ref[...] = found_ref[...]
    scan_pair(
        best_ref, own_ref, left_ref, rows_ref[0:1, :], rows_ref[1:2, :], codes_ref, core, me, left
    )
    store_groups(out_ref, best_ref[...], mine_ref[...], spots_ref[...])


def unpack_kernel(where_ref, back_ref, near_ref, far_ref, out_ref):
    half = near_ref.shape[0]
    rows = back_ref.shape[1]
    width = 2 * GROUP
    hot = (iota((2 * half, rows), 0) == back_ref[0:1, :]).astype(jnp.bfloat16)
    results = jnp.concatenate([near_ref[:, :width], far_ref[:, :width]], axis=0)
    total = jnp.zeros((width, rows), jnp.float32)
    for piece in split3(results):
        total = total + dot(piece, hot, ((0,), (0,)))
    mine = iota((width, rows), 0) == back_ref[1:2, :]
    out_ref[...] = jnp.sum(jnp.where(mine, total, 0.0), axis=0, keepdims=True)


AXES = ("dp", "help")
NY, NZ, NX = 4, 8, 4


def device(y, z, core, x):
    return ((y % NY * NZ + z % NZ) * 2 + core) * NX + x % NX


EVERY = [(y, z, c, x) for y in range(NY) for z in range(NZ) for c in range(2) for x in range(NX)]
SWAP = [(device(y, z, c, x), device(y, z, 1 - c, x)) for y, z, c, x in EVERY]
GROUPS = [[device(y, z, 0, x) for y in range(NY) for z in range(NZ)] for x in range(NX)] + [
    [device(y, z, 1, x) for z in range(NZ) for x in range(NX)] for y in range(NY)
]


def aside(step):
    return [
        (device(y, z, c, x), device(y, z, c, x + step) if c == 0 else device(y + step, z, c, x))
        for y, z, c, x in EVERY
    ]


def exchange(array):
    return lax.all_to_all(
        array, AXES, split_axis=0, concat_axis=0, axis_index_groups=GROUPS, tiled=True
    )


def shards(embeddings, clusters, send_order):
    rows, depth = embeddings.shape
    half = lax.axis_size("dp") // 2
    data = GROUP * (depth // LANES)
    dp, x = lax.axis_index("dp"), lax.axis_index("help")
    core, y = dp % 2, dp // (2 * NZ)
    where = jnp.stack([jnp.where(core == 0, x, y), core, jnp.int32(NX)])
    half_float, full_float, whole = jnp.bfloat16, jnp.float32, jnp.int32
    back, labels = call(
        rank_kernel,
        "rank",
        (where, clusters.reshape(1, rows)),
        (((8, rows), whole), ((2 * half, LANES), half_float)),
        flops=10**9,
    )
    send, notes, unit = call(
        send_kernel,
        "send",
        (where, embeddings, back, labels),
        (
            ((half, data + NOTE, LANES), half_float),
            ((half, NOTE, LANES), half_float),
            ((rows, depth), half_float),
        ),
        flops=10**9,
    )
    got = lax.ppermute(send, AXES, SWAP)
    (keep,) = call(
        keep_kernel, "keep", (where, unit, back), (((half, data, LANES), half_float),), flops=10**9
    )
    outgoing = jnp.concatenate([keep, got[:, :data], notes + got[:, data:]], axis=1)
    own = exchange(outgoing)
    left, right = lax.ppermute(own, AXES, aside(1)), lax.ppermute(own, AXES, aside(-1))
    row, lines = ((1, rows), full_float), ((8, rows), full_float)
    codes, groups = ((rows, LANES), full_float), ((half, LANES), full_float)
    spot_kind, cell_kind = ((rows, LANES), half_float), ((rows, half), half_float)
    best, own_rows, back, spots, cells, mine, left_orders, right_orders = call(
        alone_kernel,
        "alone",
        (where, own, back),
        (row, lines, ((8, rows), whole), spot_kind, cell_kind, ((half, rows), half_float), codes, codes),
        (codes,),
        10**9,
    )
    best, right_rows = call(
        right_kernel,
        "right",
        (where, best, own, right, own_rows, right_orders, spots, cells),
        (row, lines),
        (codes,),
        10**9,
    )
    cross, left_codes = call(
        cross_kernel,
        "cross",
        (where, left, right, right_rows, left_orders, spots, cells, mine),
        (groups, codes),
        (row,),
        10**9,
    )
    cross = lax.ppermute(cross, AXES, aside(1))
    (best,) = call(
        left_kernel,
        "left",
        (where, best, own, left, own_rows, left_codes, spots, mine),
        (groups,),
        (row,),
        10**9,
    )
    best = jnp.maximum(best, cross)
    near = exchange(best.reshape(half, 1, LANES)).reshape(half, LANES)
    far = lax.ppermute(near, AXES, SWAP)
    (out,) = call(unpack_kernel, "unpack", (where, back, near, far), (row,))
    return out.reshape(rows)


def solution(mesh):
    return jax.shard_map(
        shards,
        mesh=mesh,
        in_specs=(P(("dp", "help"), None), P(("dp", "help")), P(("dp", "help"))),
        out_specs=P(("dp", "help")),
        check_vma=False,
    )
```

```python
import jax
import jax.numpy as jnp
from jax import lax
from jax.experimental import pallas as pl
from jax.experimental.pallas import tpu as pltpu
from jax.sharding import PartitionSpec as P

LANES = 128
TILE = 256


def split3(x):
    high = x.astype(jnp.bfloat16)
    rest = x - high.astype(jnp.float32)
    mid = rest.astype(jnp.bfloat16)
    low = (rest - mid.astype(jnp.float32)).astype(jnp.bfloat16)
    return high, mid, low


def iota(shape, dim):
    return lax.broadcasted_iota(jnp.int32, shape, dim)


def dot(a, b, dims):
    return lax.dot_general(a, b, (dims, ((), ())), preferred_element_type=jnp.float32)


BITS = 4096.0
GROUP = 16
NOTE = 8


def slot_of(clusters, core, half):
    owner = clusters // 2
    away = jnp.where(owner // half == core, 0, 1)
    return owner % half + away * half, away


def smem():
    return pl.BlockSpec(memory_space=pltpu.SMEM)


def vmem():
    return pl.BlockSpec(memory_space=pltpu.VMEM)


def call(kernel, name, ins, outs, scratch=(), flops=0):
    return pl.pallas_call(
        kernel,
        out_shape=tuple(jax.ShapeDtypeStruct(shape, kind) for shape, kind in outs),
        in_specs=[smem()] + [vmem()] * (len(ins) - 1),
        out_specs=(vmem(),) * len(outs),
        scratch_shapes=[pltpu.VMEM(shape, kind) for shape, kind in scratch],
        compiler_params=pltpu.CompilerParams(vmem_limit_bytes=48 * 2**20),
        cost_estimate=pl.CostEstimate(flops=flops, bytes_accessed=2**20, transcendentals=0),
        name=name,
    )(*ins)


def put_rows(out_ref, unit_ref, place, base):
    rows = unit_ref.shape[0]
    each = TILE // GROUP
    for start in range(0, rows // 2, TILE):
        pick = (iota((TILE, rows), 0) + (base + start) == place).astype(jnp.bfloat16)
        block = dot(pick, unit_ref[...], ((1,), (0,))).astype(jnp.bfloat16)
        first = start // GROUP
        for lane in range(block.shape[1] // LANES):
            out_ref[first : first + each, lane * GROUP : (lane + 1) * GROUP, :] = block[
                :, lane * LANES : (lane + 1) * LANES
            ].reshape(each, GROUP, LANES)


def rank_kernel(where_ref, clu_ref, rows_ref, labels_ref):
    half = labels_ref.shape[0] // 2
    rows = clu_ref.shape[1]
    clusters = clu_ref[...]
    slot, away = slot_of(clusters, where_ref[1], half)
    hot = (iota((2 * half, rows), 0) == slot).astype(jnp.bfloat16)
    before = (iota((rows, rows), 0) < iota((rows, rows), 1)).astype(jnp.bfloat16)
    count = dot(hot, before, ((1,), (0,)))
    rank = jnp.sum(hot.astype(jnp.float32) * count, axis=0, keepdims=True).astype(jnp.int32)
    spot = rank + away * GROUP
    place = slot * GROUP + rank
    rows_ref[...] = jnp.concatenate([slot, spot, place, place] * 2, axis=0)
    bit = (clusters % 2).astype(jnp.float32)
    spots = jnp.where(iota((LANES, rows), 0) == spot, bit, 0.0).astype(jnp.bfloat16)
    labels_ref[...] = dot(hot, spots, ((1,), (1,))).astype(jnp.bfloat16)


def send_kernel(where_ref, emb_ref, rows_ref, labels_ref, send_ref, notes_ref, unit_ref):
    rows = emb_ref.shape[0]
    half = send_ref.shape[0]
    labels = labels_ref[...]
    notes_ref[...] = jnp.broadcast_to(labels[:half, None, :], (half, NOTE, LANES))
    values = emb_ref[...].astype(jnp.float32)
    scale = lax.rsqrt(jnp.sum(values * values, axis=1, keepdims=True) + 1e-06)
    unit_ref[...] = (values * scale).astype(jnp.bfloat16)
    put_rows(send_ref, unit_ref, rows_ref[2:3, :], rows // 2)
    data = send_ref.shape[1] - NOTE
    send_ref[:, data:, :] = jnp.broadcast_to(labels[half:, None, :], (half, NOTE, LANES))


def keep_kernel(where_ref, unit_ref, rows_ref, keep_ref):
    put_rows(keep_ref, unit_ref, rows_ref[2:3, :], 0)


def source_of(place):
    return place // TILE * (TILE // (2 * GROUP)) + place % (TILE // 2) // GROUP


def lane_of(place):
    return place // (TILE // 2) % 2 * GROUP + place % GROUP


def order_of(place, core, part):
    source, flip, rank = source_of(place), place // (TILE // 2) % 2, place % GROUP
    from_core = jnp.where(flip == 0, core, 1 - core)
    by_row = (source * 2 + from_core) * 4 + part
    by_column = ((part * 8 + source // 4) * 2 + from_core) * 4 + source % 4
    return jnp.where(core == 0, by_row, by_column) * GROUP + rank


def tile_of(ref, index):
    each = TILE // (2 * GROUP)
    data = (ref.shape[1] - NOTE) // 2
    here = slice(index * each, (index + 1) * each)
    lanes = []
    for base in range(0, data, GROUP):
        parts = [
            ref[here, start : start + GROUP, :].reshape(TILE // 2, LANES)
            for start in (base, data + base)
        ]
        lanes.append(jnp.concatenate(parts, axis=0))
    return jnp.concatenate(lanes, axis=1)


def notes_of(ref):
    data = ref.shape[1] - NOTE
    return (jnp.sum(ref[:, data:, :].astype(jnp.float32), axis=1) * (1.0 / NOTE)).astype(jnp.bfloat16)


def row_codes(lab, rows, core, part):
    sources = lab.shape[0]
    width = 2 * GROUP
    place = iota((1, rows), 1)
    hot = (iota((sources, rows), 0) == source_of(place)).astype(jnp.bfloat16)
    spread = dot(lab[:, :width], hot, ((0,), (0,)))
    chosen = iota((width, rows), 0) == lane_of(place)
    label = jnp.sum(jnp.where(chosen, spread, 0.0), axis=0, keepdims=True)
    return label * BITS, label * BITS + order_of(place, core, part).astype(jnp.float32)


def column_orders(rows, core, part):
    place = iota((rows, LANES), 0)
    return order_of(place, core, part).astype(jnp.float32)


def spots_of(rows):
    return (iota((rows, LANES), 1) == lane_of(iota((rows, 1), 0))).astype(jnp.bfloat16)


def cells_of(rows, sources):
    return (iota((rows, sources), 1) == source_of(iota((rows, 1), 0))).astype(jnp.bfloat16)


def mine_of(sources, rows):
    return (iota((sources, rows), 0) == source_of(iota((1, rows), 1))).astype(jnp.bfloat16)


def column_codes(lab, orders, cells, spots):
    kept = dot(cells, lab, ((1,), (0,))).astype(jnp.bfloat16) * spots
    label = dot(kept, jnp.ones((LANES, LANES), jnp.bfloat16), ((1,), (0,)))
    return label * BITS + orders


def scan(best_ref, query_ref, key_ref, floor, ceiling, codes_ref, pick):
    tiles = best_ref.shape[1] // TILE
    for query in range(tiles):
        queries = tile_of(query_ref, query)
        here = slice(query * TILE, (query + 1) * TILE)
        best = best_ref[:, here]
        for key in range(tiles):
            if not pick(key, query):
                continue
            sims = dot(tile_of(key_ref, key), queries, ((1,), (1,)))
            codes = codes_ref[key * TILE : (key + 1) * TILE, :]
            codes = jnp.concatenate([codes] * (TILE // LANES), axis=1)
            mask = (codes >= floor[:, here]) & (codes < ceiling[:, here])
            found = jnp.max(jnp.where(mask, sims, -1.0), axis=0, keepdims=True)
            best = jnp.maximum(best, found)
        best_ref[:, here] = best


def scan_pair(best_ref, query_ref, key_ref, floor, ceiling, codes_ref, core, part, key_part):
    args = (best_ref, query_ref, key_ref, floor, ceiling, codes_ref)

    @pl.when((core == 0) | (key_part < part))
    def _():
        scan(*args, lambda key, query: key <= query)

    @pl.when((core != 0) & (key_part < part))
    def _():
        scan(*args, lambda key, query: key > query)


def store_groups(out_ref, best, mine, spots):
    sources = out_ref.shape[0]
    spread = jnp.concatenate([mine * piece for piece in split3(best)], axis=0)
    total = dot(spread, spots, ((1,), (0,)))
    out_ref[...] = total[:sources] + total[sources : 2 * sources] + total[2 * sources :]


def parts_of(where_ref):
    me, core, parts = where_ref[0], where_ref[1], where_ref[2]
    return core, me, lax.rem(me + parts - 1, parts), lax.rem(me + 1, parts)


def alone_kernel(
    where_ref, own_ref, back_ref, best_ref, rows_ref, hot_ref, mark_ref, spots_ref, cells_ref, mine_ref,
    left_orders_ref, right_orders_ref, codes_ref,
):
    rows = best_ref.shape[1]
    sources = own_ref.shape[0]
    spots_ref[...] = spots_of(rows)
    cells_ref[...] = cells_of(rows, sources)
    mine_ref[...] = mine_of(sources, rows)
    core, me, left, right = parts_of(where_ref)
    left_orders_ref[...] = column_orders(rows, core, left)
    right_orders_ref[...] = column_orders(rows, core, right)
    hot_ref[...] = (iota(hot_ref.shape, 0) == back_ref[0:1, :]).astype(jnp.bfloat16)
    mark_ref[...] = (iota(mark_ref.shape, 0) == back_ref[1:2, :]).astype(jnp.float32)
    lab = notes_of(own_ref)
    floor, ceiling = row_codes(lab, rows, core, me)
    rows_ref[...] = jnp.concatenate([floor, ceiling] * 4, axis=0)
    codes_ref[...] = column_codes(lab, column_orders(rows, core, me), cells_ref[...], spots_ref[...])
    best_ref[...] = jnp.full((1, rows), -1.0, jnp.float32)
    scan(best_ref, own_ref, own_ref, floor, ceiling, codes_ref, lambda key, query: key <= query)


def right_kernel(
    where_ref, alone_ref, own_ref, right_ref, rows_ref, orders_ref, spots_ref, cells_ref,
    best_ref, right_rows_ref, codes_ref,
):
    rows = best_ref.shape[1]
    core, me, _, right = parts_of(where_ref)
    best_ref[...] = alone_ref[...]
    lab = notes_of(right_ref)
    floor, ceiling = row_codes(lab, rows, core, right)
    right_rows_ref[...] = jnp.concatenate([floor, ceiling] * 4, axis=0)
    codes_ref[...] = column_codes(lab, orders_ref[...], cells_ref[...], spots_ref[...])
    scan_pair(
        best_ref, own_ref, right_ref, rows_ref[0:1, :], rows_ref[1:2, :], codes_ref, core, me, right
    )


def cross_kernel(
    where_ref, left_ref, right_ref, rows_ref, orders_ref, spots_ref, cells_ref, mine_ref,
    out_ref, codes_ref, best_ref,
):
    rows = best_ref.shape[1]
    core, _, left, right = parts_of(where_ref)
    codes_ref[...] = column_codes(notes_of(left_ref), orders_ref[...], cells_ref[...], spots_ref[...])
    best_ref[...] = jnp.full((1, rows), -1.0, jnp.float32)
    scan_pair(
        best_ref, right_ref, left_ref, rows_ref[0:1, :], rows_ref[1:2, :], codes_ref, core, right, left
    )
    store_groups(out_ref, best_ref[...], mine_ref[...], spots_ref[...])


def left_kernel(
    where_ref, found_ref, own_ref, left_ref, rows_ref, codes_ref, spots_ref, mine_ref, out_ref, best_ref
):
    core, me, left, _ = parts_of(where_ref)
    best_ref[...] = found_ref[...]
    scan_pair(
        best_ref, own_ref, left_ref, rows_ref[0:1, :], rows_ref[1:2, :], codes_ref, core, me, left
    )
    store_groups(out_ref, best_ref[...], mine_ref[...], spots_ref[...])


def unpack_kernel(where_ref, hot_ref, mine_ref, near_ref, far_ref, out_ref):
    width = mine_ref.shape[0]
    results = jnp.concatenate([near_ref[:, :width], far_ref[:, :width]], axis=0)
    pieces = jnp.concatenate(split3(results), axis=1)
    total = dot(pieces, hot_ref[...], ((0,), (0,)))
    total = total[:width] + total[width : 2 * width] + total[2 * width :]
    out_ref[...] = jnp.sum(total * mine_ref[...], axis=0, keepdims=True)


AXES = ("dp", "help")
NY, NZ, NX = 4, 8, 4


def device(y, z, core, x):
    return ((y % NY * NZ + z % NZ) * 2 + core) * NX + x % NX


EVERY = [(y, z, c, x) for y in range(NY) for z in range(NZ) for c in range(2) for x in range(NX)]
SWAP = [(device(y, z, c, x), device(y, z, 1 - c, x)) for y, z, c, x in EVERY]
GROUPS = [[device(y, z, 0, x) for y in range(NY) for z in range(NZ)] for x in range(NX)] + [
    [device(y, z, 1, x) for z in range(NZ) for x in range(NX)] for y in range(NY)
]


def aside(step):
    return [
        (device(y, z, c, x), device(y, z, c, x + step) if c == 0 else device(y + step, z, c, x))
        for y, z, c, x in EVERY
    ]


def exchange(array):
    return lax.all_to_all(
        array, AXES, split_axis=0, concat_axis=0, axis_index_groups=GROUPS, tiled=True
    )


def shards(embeddings, clusters, send_order):
    rows, depth = embeddings.shape
    half = lax.axis_size("dp") // 2
    data = GROUP * (depth // LANES)
    dp, x = lax.axis_index("dp"), lax.axis_index("help")
    core, y = dp % 2, dp // (2 * NZ)
    where = jnp.stack([jnp.where(core == 0, x, y), core, jnp.int32(NX)])
    half_float, full_float, whole = jnp.bfloat16, jnp.float32, jnp.int32
    back, labels = call(
        rank_kernel,
        "rank",
        (where, clusters.reshape(1, rows)),
        (((8, rows), whole), ((2 * half, LANES), half_float)),
        flops=10**9,
    )
    send, notes, unit = call(
        send_kernel,
        "send",
        (where, embeddings, back, labels),
        (
            ((half, data + NOTE, LANES), half_float),
            ((half, NOTE, LANES), half_float),
            ((rows, depth), half_float),
        ),
        flops=10**9,
    )
    got = lax.ppermute(send, AXES, SWAP)
    (keep,) = call(
        keep_kernel, "keep", (where, unit, back), (((half, data, LANES), half_float),), flops=10**9
    )
    outgoing = jnp.concatenate([keep, got[:, :data], notes + got[:, data:]], axis=1)
    own = exchange(outgoing)
    left, right = lax.ppermute(own, AXES, aside(1)), lax.ppermute(own, AXES, aside(-1))
    row, lines = ((1, rows), full_float), ((8, rows), full_float)
    codes, groups = ((rows, LANES), full_float), ((half, LANES), full_float)
    spot_kind, cell_kind = ((rows, LANES), half_float), ((rows, half), half_float)
    best, own_rows, hot, marks, spots, cells, mine, left_orders, right_orders = call(
        alone_kernel,
        "alone",
        (where, own, back),
        (row, lines, ((2 * half, rows), half_float), ((2 * GROUP, rows), full_float), spot_kind, cell_kind, ((half, rows), half_float), codes, codes),
        (codes,),
        10**9,
    )
    best, right_rows = call(
        right_kernel,
        "right",
        (where, best, own, right, own_rows, right_orders, spots, cells),
        (row, lines),
        (codes,),
        10**9,
    )
    cross, left_codes = call(
        cross_kernel,
        "cross",
        (where, left, right, right_rows, left_orders, spots, cells, mine),
        (groups, codes),
        (row,),
        10**9,
    )
    cross = lax.ppermute(cross, AXES, aside(1))
    (best,) = call(
        left_kernel,
        "left",
        (where, best, own, left, own_rows, left_codes, spots, mine),
        (groups,),
        (row,),
        10**9,
    )
    best = jnp.maximum(best, cross)
    near = exchange(best.reshape(half, 1, LANES)).reshape(half, LANES)
    far = lax.ppermute(near, AXES, SWAP)
    (out,) = call(unpack_kernel, "unpack", (where, hot, marks, near, far), (row,))
    return out.reshape(rows)


def solution(mesh):
    return jax.shard_map(
        shards,
        mesh=mesh,
        in_specs=(P(("dp", "help"), None), P(("dp", "help")), P(("dp", "help"))),
        out_specs=P(("dp", "help")),
        check_vma=False,
    )
```

```python
import jax
import jax.numpy as jnp
from jax import lax
from jax.experimental import pallas as pl
from jax.experimental.pallas import tpu as pltpu
from jax.sharding import PartitionSpec as P

LANES = 128
TILE = 256


def split3(x):
    high = x.astype(jnp.bfloat16)
    rest = x - high.astype(jnp.float32)
    mid = rest.astype(jnp.bfloat16)
    low = (rest - mid.astype(jnp.float32)).astype(jnp.bfloat16)
    return high, mid, low


def iota(shape, dim):
    return lax.broadcasted_iota(jnp.int32, shape, dim)


def dot(a, b, dims):
    return lax.dot_general(a, b, (dims, ((), ())), preferred_element_type=jnp.float32)


BITS = 4096.0
GROUP = 16
NOTE = 8


def slot_of(clusters, core, half):
    owner = clusters // 2
    away = jnp.where(owner // half == core, 0, 1)
    return owner % half + away * half, away


def smem():
    return pl.BlockSpec(memory_space=pltpu.SMEM)


def vmem():
    return pl.BlockSpec(memory_space=pltpu.VMEM)


def call(kernel, name, ins, outs, scratch=(), flops=0):
    return pl.pallas_call(
        kernel,
        out_shape=tuple(jax.ShapeDtypeStruct(shape, kind) for shape, kind in outs),
        in_specs=[smem()] + [vmem()] * (len(ins) - 1),
        out_specs=(vmem(),) * len(outs),
        scratch_shapes=[pltpu.VMEM(shape, kind) for shape, kind in scratch],
        compiler_params=pltpu.CompilerParams(vmem_limit_bytes=48 * 2**20),
        cost_estimate=pl.CostEstimate(flops=flops, bytes_accessed=2**20, transcendentals=0),
        name=name,
    )(*ins)


def put_rows(out_ref, unit_ref, place, base):
    rows = unit_ref.shape[0]
    size = rows // 2
    each = size // GROUP
    for start in range(0, size, size):
        pick = (iota((size, rows), 0) + (base + start) == place).astype(jnp.bfloat16)
        block = dot(pick, unit_ref[...], ((1,), (0,))).astype(jnp.bfloat16)
        first = start // GROUP
        for lane in range(block.shape[1] // LANES):
            out_ref[first : first + each, lane * GROUP : (lane + 1) * GROUP, :] = block[
                :, lane * LANES : (lane + 1) * LANES
            ].reshape(each, GROUP, LANES)


def rank_kernel(where_ref, clu_ref, rows_ref, labels_ref):
    half = labels_ref.shape[0] // 2
    rows = clu_ref.shape[1]
    clusters = clu_ref[...]
    slot, away = slot_of(clusters, where_ref[1], half)
    hot = (iota((2 * half, rows), 0) == slot).astype(jnp.bfloat16)
    before = (iota((rows, rows), 0) < iota((rows, rows), 1)).astype(jnp.bfloat16)
    count = dot(hot, before, ((1,), (0,)))
    rank = jnp.sum(hot.astype(jnp.float32) * count, axis=0, keepdims=True).astype(jnp.int32)
    spot = rank + away * GROUP
    place = slot * GROUP + rank
    rows_ref[...] = jnp.concatenate([slot, spot, place, place] * 2, axis=0)
    bit = (clusters % 2).astype(jnp.float32)
    spots = jnp.where(iota((LANES, rows), 0) == spot, bit, 0.0).astype(jnp.bfloat16)
    labels_ref[...] = dot(hot, spots, ((1,), (1,))).astype(jnp.bfloat16)


def send_kernel(where_ref, emb_ref, rows_ref, labels_ref, send_ref, notes_ref, unit_ref):
    rows = emb_ref.shape[0]
    half = send_ref.shape[0]
    labels = labels_ref[...]
    notes_ref[...] = jnp.broadcast_to(labels[:half, None, :], (half, NOTE, LANES))
    values = emb_ref[...].astype(jnp.float32)
    scale = lax.rsqrt(jnp.sum(values * values, axis=1, keepdims=True) + 1e-06)
    unit_ref[...] = (values * scale).astype(jnp.bfloat16)
    put_rows(send_ref, unit_ref, rows_ref[2:3, :], rows // 2)
    data = send_ref.shape[1] - NOTE
    send_ref[:, data:, :] = jnp.broadcast_to(labels[half:, None, :], (half, NOTE, LANES))


def keep_kernel(where_ref, unit_ref, rows_ref, keep_ref):
    put_rows(keep_ref, unit_ref, rows_ref[2:3, :], 0)


def source_of(place):
    return place // TILE * (TILE // (2 * GROUP)) + place % (TILE // 2) // GROUP


def lane_of(place):
    return place // (TILE // 2) % 2 * GROUP + place % GROUP


def order_of(place, core, part):
    source, flip, rank = source_of(place), place // (TILE // 2) % 2, place % GROUP
    from_core = jnp.where(flip == 0, core, 1 - core)
    by_row = (source * 2 + from_core) * 4 + part
    by_column = ((part * 8 + source // 4) * 2 + from_core) * 4 + source % 4
    return jnp.where(core == 0, by_row, by_column) * GROUP + rank


def tile_of(ref, index):
    each = TILE // (2 * GROUP)
    data = (ref.shape[1] - NOTE) // 2
    here = slice(index * each, (index + 1) * each)
    lanes = []
    for base in range(0, data, GROUP):
        parts = [
            ref[here, start : start + GROUP, :].reshape(TILE // 2, LANES)
            for start in (base, data + base)
        ]
        lanes.append(jnp.concatenate(parts, axis=0))
    return jnp.concatenate(lanes, axis=1)


def notes_of(ref):
    data = ref.shape[1] - NOTE
    return (jnp.sum(ref[:, data:, :].astype(jnp.float32), axis=1) * (1.0 / NOTE)).astype(jnp.bfloat16)


def row_codes(lab, rows, core, part):
    sources = lab.shape[0]
    width = 2 * GROUP
    place = iota((1, rows), 1)
    hot = (iota((sources, rows), 0) == source_of(place)).astype(jnp.bfloat16)
    spread = dot(lab[:, :width], hot, ((0,), (0,)))
    chosen = iota((width, rows), 0) == lane_of(place)
    label = jnp.sum(jnp.where(chosen, spread, 0.0), axis=0, keepdims=True)
    return label * BITS, label * BITS + order_of(place, core, part).astype(jnp.float32)


def column_orders(rows, core, part):
    place = iota((rows, LANES), 0)
    return order_of(place, core, part).astype(jnp.float32)


def spots_of(rows):
    return (iota((rows, LANES), 1) == lane_of(iota((rows, 1), 0))).astype(jnp.bfloat16)


def cells_of(rows, sources):
    return (iota((rows, sources), 1) == source_of(iota((rows, 1), 0))).astype(jnp.bfloat16)


def mine_of(sources, rows):
    return (iota((sources, rows), 0) == source_of(iota((1, rows), 1))).astype(jnp.bfloat16)


def column_codes(lab, orders, cells, spots):
    kept = dot(cells, lab, ((1,), (0,))).astype(jnp.bfloat16) * spots
    label = dot(kept, jnp.ones((LANES, LANES), jnp.bfloat16), ((1,), (0,)))
    return label * BITS + orders


def scan(best_ref, query_ref, key_ref, floor, ceiling, codes_ref, pick):
    tiles = best_ref.shape[1] // TILE
    for query in range(tiles):
        queries = tile_of(query_ref, query)
        here = slice(query * TILE, (query + 1) * TILE)
        best = best_ref[:, here]
        for key in range(tiles):
            if not pick(key, query):
                continue
            sims = dot(tile_of(key_ref, key), queries, ((1,), (1,)))
            codes = codes_ref[key * TILE : (key + 1) * TILE, :]
            codes = jnp.concatenate([codes] * (TILE // LANES), axis=1)
            mask = (codes >= floor[:, here]) & (codes < ceiling[:, here])
            found = jnp.max(jnp.where(mask, sims, -1.0), axis=0, keepdims=True)
            best = jnp.maximum(best, found)
        best_ref[:, here] = best


def scan_pair(best_ref, query_ref, key_ref, floor, ceiling, codes_ref, core, part, key_part):
    args = (best_ref, query_ref, key_ref, floor, ceiling, codes_ref)

    @pl.when((core == 0) | (key_part < part))
    def _():
        scan(*args, lambda key, query: key <= query)

    @pl.when((core != 0) & (key_part < part))
    def _():
        scan(*args, lambda key, query: key > query)


def store_groups(out_ref, best, mine, spots):
    sources = out_ref.shape[0]
    spread = jnp.concatenate([mine * piece for piece in split3(best)], axis=0)
    total = dot(spread, spots, ((1,), (0,)))
    out_ref[...] = total[:sources] + total[sources : 2 * sources] + total[2 * sources :]


def parts_of(where_ref):
    me, core, parts = where_ref[0], where_ref[1], where_ref[2]
    return core, me, lax.rem(me + parts - 1, parts), lax.rem(me + 1, parts)


def alone_kernel(
    where_ref, own_ref, back_ref, best_ref, rows_ref, kept_ref, spots_ref, cells_ref, mine_ref,
    left_orders_ref, right_orders_ref, codes_ref,
):
    rows = best_ref.shape[1]
    sources = own_ref.shape[0]
    spots_ref[...] = spots_of(rows)
    cells_ref[...] = cells_of(rows, sources)
    mine_ref[...] = mine_of(sources, rows)
    core, me, left, right = parts_of(where_ref)
    left_orders_ref[...] = column_orders(rows, core, left)
    right_orders_ref[...] = column_orders(rows, core, right)
    kept_ref[...] = back_ref[...]
    lab = notes_of(own_ref)
    floor, ceiling = row_codes(lab, rows, core, me)
    rows_ref[...] = jnp.concatenate([floor, ceiling] * 4, axis=0)
    codes_ref[...] = column_codes(lab, column_orders(rows, core, me), cells_ref[...], spots_ref[...])
    best_ref[...] = jnp.full((1, rows), -1.0, jnp.float32)
    scan(best_ref, own_ref, own_ref, floor, ceiling, codes_ref, lambda key, query: key <= query)


def right_kernel(
    where_ref, alone_ref, own_ref, right_ref, rows_ref, orders_ref, spots_ref, cells_ref,
    best_ref, right_rows_ref, codes_ref,
):
    rows = best_ref.shape[1]
    core, me, _, right = parts_of(where_ref)
    best_ref[...] = alone_ref[...]
    lab = notes_of(right_ref)
    floor, ceiling = row_codes(lab, rows, core, right)
    right_rows_ref[...] = jnp.concatenate([floor, ceiling] * 4, axis=0)
    codes_ref[...] = column_codes(lab, orders_ref[...], cells_ref[...], spots_ref[...])
    scan_pair(
        best_ref, own_ref, right_ref, rows_ref[0:1, :], rows_ref[1:2, :], codes_ref, core, me, right
    )


def cross_kernel(
    where_ref, left_ref, right_ref, rows_ref, orders_ref, spots_ref, cells_ref, mine_ref,
    out_ref, codes_ref, best_ref,
):
    rows = best_ref.shape[1]
    core, _, left, right = parts_of(where_ref)
    codes_ref[...] = column_codes(notes_of(left_ref), orders_ref[...], cells_ref[...], spots_ref[...])
    best_ref[...] = jnp.full((1, rows), -1.0, jnp.float32)
    scan_pair(
        best_ref, right_ref, left_ref, rows_ref[0:1, :], rows_ref[1:2, :], codes_ref, core, right, left
    )
    store_groups(out_ref, best_ref[...], mine_ref[...], spots_ref[...])


def left_kernel(
    where_ref, found_ref, own_ref, left_ref, rows_ref, codes_ref, spots_ref, mine_ref, out_ref, best_ref
):
    core, me, left, _ = parts_of(where_ref)
    best_ref[...] = found_ref[...]
    scan_pair(
        best_ref, own_ref, left_ref, rows_ref[0:1, :], rows_ref[1:2, :], codes_ref, core, me, left
    )
    store_groups(out_ref, best_ref[...], mine_ref[...], spots_ref[...])


def unpack_kernel(where_ref, back_ref, near_ref, far_ref, out_ref):
    half = near_ref.shape[0]
    rows = back_ref.shape[1]
    width = 2 * GROUP
    hot = (iota((2 * half, rows), 0) == back_ref[0:1, :]).astype(jnp.bfloat16)
    results = jnp.concatenate([near_ref[:, :width], far_ref[:, :width]], axis=0)
    total = jnp.zeros((width, rows), jnp.float32)
    for piece in split3(results):
        total = total + dot(piece, hot, ((0,), (0,)))
    mine = iota((width, rows), 0) == back_ref[1:2, :]
    out_ref[...] = jnp.sum(jnp.where(mine, total, 0.0), axis=0, keepdims=True)


AXES = ("dp", "help")
NY, NZ, NX = 4, 8, 4


def device(y, z, core, x):
    return ((y % NY * NZ + z % NZ) * 2 + core) * NX + x % NX


EVERY = [(y, z, c, x) for y in range(NY) for z in range(NZ) for c in range(2) for x in range(NX)]
SWAP = [(device(y, z, c, x), device(y, z, 1 - c, x)) for y, z, c, x in EVERY]
GROUPS = [[device(y, z, 0, x) for y in range(NY) for z in range(NZ)] for x in range(NX)] + [
    [device(y, z, 1, x) for z in range(NZ) for x in range(NX)] for y in range(NY)
]


def aside(step):
    return [
        (device(y, z, c, x), device(y, z, c, x + step) if c == 0 else device(y + step, z, c, x))
        for y, z, c, x in EVERY
    ]


def exchange(array):
    return lax.all_to_all(
        array, AXES, split_axis=0, concat_axis=0, axis_index_groups=GROUPS, tiled=True
    )


def shards(embeddings, clusters, send_order):
    rows, depth = embeddings.shape
    half = lax.axis_size("dp") // 2
    data = GROUP * (depth // LANES)
    dp, x = lax.axis_index("dp"), lax.axis_index("help")
    core, y = dp % 2, dp // (2 * NZ)
    where = jnp.stack([jnp.where(core == 0, x, y), core, jnp.int32(NX)])
    half_float, full_float, whole = jnp.bfloat16, jnp.float32, jnp.int32
    back, labels = call(
        rank_kernel,
        "rank",
        (where, clusters.reshape(1, rows)),
        (((8, rows), whole), ((2 * half, LANES), half_float)),
        flops=10**9,
    )
    send, notes, unit = call(
        send_kernel,
        "send",
        (where, embeddings, back, labels),
        (
            ((half, data + NOTE, LANES), half_float),
            ((half, NOTE, LANES), half_float),
            ((rows, depth), half_float),
        ),
        flops=10**9,
    )
    got = lax.ppermute(send, AXES, SWAP)
    (keep,) = call(
        keep_kernel, "keep", (where, unit, back), (((half, data, LANES), half_float),), flops=10**9
    )
    outgoing = jnp.concatenate([keep, got[:, :data], notes + got[:, data:]], axis=1)
    own = exchange(outgoing)
    left, right = lax.ppermute(own, AXES, aside(1)), lax.ppermute(own, AXES, aside(-1))
    row, lines = ((1, rows), full_float), ((8, rows), full_float)
    codes, groups = ((rows, LANES), full_float), ((half, LANES), full_float)
    spot_kind, cell_kind = ((rows, LANES), half_float), ((rows, half), half_float)
    best, own_rows, back, spots, cells, mine, left_orders, right_orders = call(
        alone_kernel,
        "alone",
        (where, own, back),
        (row, lines, ((8, rows), whole), spot_kind, cell_kind, ((half, rows), half_float), codes, codes),
        (codes,),
        10**9,
    )
    best, right_rows = call(
        right_kernel,
        "right",
        (where, best, own, right, own_rows, right_orders, spots, cells),
        (row, lines),
        (codes,),
        10**9,
    )
    cross, left_codes = call(
        cross_kernel,
        "cross",
        (where, left, right, right_rows, left_orders, spots, cells, mine),
        (groups, codes),
        (row,),
        10**9,
    )
    cross = lax.ppermute(cross, AXES, aside(1))
    (best,) = call(
        left_kernel,
        "left",
        (where, best, own, left, own_rows, left_codes, spots, mine),
        (groups,),
        (row,),
        10**9,
    )
    best = jnp.maximum(best, cross)
    near = exchange(best.reshape(half, 1, LANES)).reshape(half, LANES)
    far = lax.ppermute(near, AXES, SWAP)
    (out,) = call(unpack_kernel, "unpack", (where, back, near, far), (row,))
    return out.reshape(rows)


def solution(mesh):
    return jax.shard_map(
        shards,
        mesh=mesh,
        in_specs=(P(("dp", "help"), None), P(("dp", "help")), P(("dp", "help"))),
        out_specs=P(("dp", "help")),
        check_vma=False,
    )
```
